32 devices in a mesh: group: 2 (over x), afd: 8 (over z, y), tensor: 2 (over core).
Axes of the slice: x: 2, y: 2, z: 4, core: 2. Of those that a mesh axis runs over, the one named last changes fastest.
Arguments:
- kv_cache: bfloat16 [896, 64, 576], P(('group', 'afd')), parts along dimension 0, may hold values from -6 to 6
- queries: bfloat16 [768, 64, 576], P(('group', 'afd'), 'tensor'), parts along dimension 0, may hold values from -64 to 64
- stream: bfloat16 [768, 7168], P('group', 'afd'), parts along dimension 0, may hold values from -3 to 3
- page_table: int32 [768, 8], P(('group', 'afd')), parts along dimension 0, may hold values from 0 to 55, as said below
- lengths: int32 [768], P(('group', 'afd')), parts along dimension 0, may hold values from 1 to 512, as said below
- send_pages: int32 [128, 2], P(('group', 'afd')), parts along dimension 0, may hold values from 40 to 55, as said below
- routes: int32 [768, 1], P('group'), parts along dimension 0, may hold values from 0 to 3; in each aligned block of 384 rows (0 to 383, 384 to 767, ...) at most 240 rows name the same one
- value_up: bfloat16 [64, 512, 128], P('tensor'), may hold values from -0.75 to 0.75
- output_weight: bfloat16 [8192, 7168], P('tensor', 'afd'), may hold values from -0.125 to 0.125
- norm_gain: float32 [7168], replicated, may hold values from 0.1 to 1.9
- gate_weight: bfloat16 [7168, 4096], P(None, ('afd', 'tensor')), may hold values from -0.0625 to 0.0625
- up_weight: bfloat16 [7168, 4096], P(None, ('afd', 'tensor')), may hold values from -0.0625 to 0.0625
- down_weight: bfloat16 [4096, 7168], P(('afd', 'tensor')), may hold values from -0.1875 to 0.1875
Outputs:
- mixed: bfloat16 [768, 7168], P('group', ('afd', 'tensor')), parts along dimension 0
The draws below stay inside these ranges and needn't reach their ends.
There are 2 independent parts, one for each index of `group`. The reference program is written for one: setup_inputs(seed, part) draws one part's arguments, and reference() takes and returns one part's arrays. A program takes and returns all parts, laid end to end along the dimension named above; an argument that names none is the same for every part. Nothing has to cross between parts.
Inputs may be any that keep to these rules, and one draw needn't show every extreme that they name: `page_table`: row i lists the slots of request i on its device. The first ceil(lengths[i] / 64) entries are distinct and the later ones repeat the last of them; every slot of a device belongs to exactly one request. `lengths`: each device has a request of exactly 512 tokens. `send_pages`: row d of device b's block lists the 2 own pages that b sends to device d; each page of b from 40 up is listed exactly once. `routes`: at most 240 tokens name one expert, a bound that some block reaches.
All inputs are finite; a program needn't handle non-finite values.
Results may differ from the reference program's by a relative error of at most 0.007.
Values may be sent and summed in bfloat16 or wider, within the bound.
A program may use at most 192 MiB of HBM per device.

```python
import math
import jax
import jax.numpy as jnp
import numpy as np
from jax import lax

D = 7168
H = 64
LAT = 512
ROPE = 64
VDIM = 128
FFH = 1024
PAGE = 64
MAXP = 8
MIG = 2
TOK_DEV = 48
TOKENS = 384
PAGES_DEV = 56
LOCAL = 40
EXPERTS = 4
CAP = 240
N_AFD = 8


def page_layout(key):
    key_count, key_long, key_slot, key_tail, key_send = jax.random.split(key, 5)
    extra = PAGES_DEV - TOK_DEV - MAXP + 1
    units = (TOK_DEV - 1) * (MAXP - 1)

    def spread(one_key):
        shuffled = jax.random.permutation(one_key, units)
        chosen = (shuffled < extra).astype(jnp.int32).reshape(TOK_DEV - 1, MAXP - 1)
        return jnp.sum(chosen, axis=1) + 1
    rest = jax.vmap(spread)(jax.random.split(key_count, N_AFD))
    longest = jax.random.randint(key_long, (N_AFD, 1), 0, TOK_DEV)
    index = jnp.arange(TOK_DEV, dtype=jnp.int32)[None, :]
    shifted = jnp.clip(index - (index > longest).astype(jnp.int32), 0, TOK_DEV - 2)
    counts = jnp.where(index == longest, MAXP, jnp.take_along_axis(rest, shifted, axis=1))
    offsets = jnp.cumsum(counts, axis=1) - counts
    slots = jax.vmap(lambda one_key: jax.random.permutation(one_key, PAGES_DEV))(jax.random.split(key_slot, N_AFD))
    page_index = jnp.arange(MAXP, dtype=jnp.int32)[None, None, :]
    within = offsets[:, :, None] + jnp.minimum(page_index, counts[:, :, None] - 1)
    table = jnp.take_along_axis(slots, within.reshape(N_AFD, TOK_DEV * MAXP), axis=1)
    table = table.reshape(N_AFD * TOK_DEV, MAXP).astype(jnp.int32)
    tail = jax.random.randint(key_tail, (N_AFD, TOK_DEV), 1, PAGE + 1)
    request_lengths = jnp.where(index == longest, MAXP * PAGE, (counts - 1) * PAGE + tail)
    request_lengths = request_lengths.reshape(N_AFD * TOK_DEV).astype(jnp.int32)
    sends = jax.vmap(lambda one_key: jax.random.permutation(one_key, N_AFD * MIG))(jax.random.split(key_send, N_AFD))
    sends = (sends + LOCAL).reshape(N_AFD * N_AFD, MIG).astype(jnp.int32)
    return (table, request_lengths, sends)


def draw_page_table(key, part):
    table, request_lengths, sends = page_layout(key)
    return table


def draw_lengths(key, part):
    table, request_lengths, sends = page_layout(key)
    return request_lengths


def draw_send_pages(key, part):
    table, request_lengths, sends = page_layout(key)
    return sends


def draw_queries(key, part):
    key = jax.random.fold_in(key, 7)
    key_base = jax.random.fold_in(key, 0)
    shape = (TOKENS, H, LAT + ROPE)
    values = jnp.clip(0.5 * jax.random.normal(key_base, shape, jnp.float32), -3.0, 3.0)
    return values.astype(jnp.bfloat16)


def levels(own_key, extent, shards, low, largest):
    def one(axis_at, parts):
        heights = jax.random.uniform(jax.random.fold_in(jax.random.fold_in(own_key, 6), axis_at), (parts,), jnp.float32, low / len(shards), largest / len(shards))
        return jnp.repeat(jnp.exp(heights), extent[axis_at] // parts).reshape((-1,) + (1,) * (len(extent) - axis_at - 1))

    loudness = one(*shards[0])
    for cut in shards[1:]:
        loudness = loudness * one(*cut)
    return loudness


def assign_block(key, own, number, rows, count, top, most, skew):
    ranking = jax.random.permutation(key, count)
    crowded, ordinary = shares(count, rows * top, most, skew, True), shares(count, rows * top, most, skew, False)
    places = jnp.arange(count)

    def named(tallies, turn):
        used = int((tallies > 0).sum())
        fixed = max(1, used // 4)
        moved = fixed + (places - fixed + turn * (used - fixed)) % max(1, count - fixed)
        return jnp.zeros((count,), jnp.int32).at[ranking[jnp.where(places < fixed, places, moved)]].set(jnp.asarray(tallies, jnp.int32))

    tallies = jnp.where(number % 4 == 0, named(crowded, number // 4), named(ordinary, number - number // 4 - 1))
    mixed = jax.random.permutation(jax.random.fold_in(own, 3), count)
    source_of, taker = mixed[0:count // 2 * 2:2], mixed[1:count // 2 * 2:2]
    margin = jnp.minimum(tallies[source_of] - 1, most - tallies[taker]) // 2
    margin = jnp.where((source_of == ranking[0]) | (taker == ranking[0]) | (tallies[taker] == 0), 0, jnp.maximum(margin, 0))
    moved = jax.random.randint(jax.random.fold_in(own, 4), (count // 2,), 0, 1 << 20) % (margin + 1)
    tallies = tallies.at[source_of].add(-moved).at[taker].add(moved)
    members = jnp.searchsorted(jnp.cumsum(tallies), jnp.arange(rows * top), side="right").astype(jnp.int32)
    table = members.reshape(top, rows).T
    table = table[jax.random.permutation(jax.random.fold_in(own, 1), rows)]
    turn = jax.random.randint(jax.random.fold_in(own, 2), (rows, 1), 0, top)
    return jnp.take_along_axis(table, (jnp.arange(top)[None, :] + turn) % top, axis=1)


def shares(number_of, total, bound, lean, full):
    weights = [(1 << 20) // math.isqrt(grade ** lean) + 1 for grade in range(1, number_of + 1)]
    largest = bound if full else min(bound, max(-(-total // number_of), total * weights[0] // sum(weights)))
    least = 1 if total - largest >= number_of - 1 else 0
    given, spare = [largest] + [least] * (number_of - 1), total - largest - least * (number_of - 1)
    while spare > 0:
        free = [i for i in range(1, number_of) if given[i] < largest] or [i for i in range(1, number_of) if given[i] < bound]
        pool, budget = sum([weights[i] for i in free]), spare
        for i in free:
            more = min(bound - given[i], max(1, budget * weights[i] // pool), spare)
            given[i] = given[i] + more
            spare = spare - more
    return np.array(given)


def scatter_about(own_key, dims, width, limit, cuts=(), held_as=jnp.bfloat16):
    array = width * jax.random.normal(own_key, dims, jnp.float32)
    if cuts:
        array = array * levels(own_key, dims, cuts, -0.22, 0.18)
    return jnp.clip(array, -limit, limit).astype(held_as)


def setup_inputs(seed: int = 0, part: int = 0) -> dict:
    key_list = jax.random.split(jax.random.key(seed), 14)
    part_keys = jax.random.split(jax.random.fold_in(key_list[13], part), 14)
    kv_cache = scatter_about(part_keys[0], (N_AFD * PAGES_DEV, PAGE, LAT + ROPE), 1.0, 6.0, ((0, 8),))
    queries = draw_queries(jax.random.fold_in(jax.random.fold_in(key_list[13], part), 71), part)
    stream = scatter_about(part_keys[2], (TOKENS, D), 0.5, 3.0, ((1, 8),))
    page_table = draw_page_table(jax.random.fold_in(jax.random.fold_in(key_list[13], part), 71), part)
    lengths = draw_lengths(jax.random.fold_in(jax.random.fold_in(key_list[13], part), 71), part)
    send_pages = draw_send_pages(jax.random.fold_in(jax.random.fold_in(key_list[13], part), 71), part)
    routes_keys = jax.random.split(jax.random.fold_in(part_keys[6], 1), TOKENS // TOKENS)
    routes_turns = jax.random.permutation(jax.random.fold_in(part_keys[6], 3), TOKENS // TOKENS)
    routes = jax.vmap(lambda own, number: assign_block(jax.random.fold_in(part_keys[6], 2), own, number, TOKENS, EXPERTS, 1, CAP, 2))(routes_keys, routes_turns).reshape((TOKENS, 1))
    value_up = scatter_about(key_list[7], (H, LAT, VDIM), (LAT // 8) ** -0.5, 0.75, ((0, 2),))
    output_weight = scatter_about(key_list[8], (H * VDIM, D), (H * VDIM // 4) ** -0.5, 0.125, ((0, 2), (1, 8)))
    norm_gain = jnp.clip(1.0 + 0.18 * jax.random.normal(key_list[9], (D,), jnp.float32), 0.1, 1.9)
    gate_weight = scatter_about(key_list[10], (D, EXPERTS * FFH), D ** -0.5, 0.0625, ((1, 16),))
    up_weight = scatter_about(key_list[11], (D, EXPERTS * FFH), D ** -0.5, 0.0625, ((1, 16),))
    down_weight = scatter_about(key_list[12], (EXPERTS * FFH, D), FFH ** -0.5, 0.1875, ((0, 16),))
    return dict(kv_cache=kv_cache, queries=queries, stream=stream, page_table=page_table, lengths=lengths, send_pages=send_pages, routes=routes, value_up=value_up, output_weight=output_weight, norm_gain=norm_gain, gate_weight=gate_weight, up_weight=up_weight, down_weight=down_weight)


score_scale = 0.07216878364870322
norm_eps = 1e-06

def resolve_keys(cache, sends, slots, device):
    resident = slots < LOCAL
    moved = jnp.maximum(slots - LOCAL, 0).astype(jnp.int32)
    source = (moved // MIG).astype(jnp.int32)
    within = (moved % MIG).astype(jnp.int32)
    remote_page = sends[source, device, within]
    owner = jnp.where(resident, device, source).astype(jnp.int32)
    page_index = jnp.where(resident, slots, remote_page).astype(jnp.int32)
    return cache[owner, page_index]

def attend(cache, sends, slots, request_lengths, query, device):
    page_keys = resolve_keys(cache, sends, slots, device).reshape(TOK_DEV, MAXP * PAGE, LAT + ROPE)
    scores = jnp.einsum('rhc,rkc->rhk', query.astype(jnp.float32), page_keys.astype(jnp.float32)) * score_scale
    position = jnp.arange(MAXP * PAGE, dtype=jnp.int32)
    valid = position[None, None, :] < request_lengths[:, None, None]
    scores = jnp.where(valid, scores, -jnp.inf)
    highest = lax.optimization_barrier(jnp.max(scores, axis=-1, keepdims=True))
    exponent = jnp.exp(scores - highest)
    weights = (exponent / lax.optimization_barrier(jnp.sum(exponent, axis=-1, keepdims=True))).astype(jnp.bfloat16)
    context = jnp.einsum('rhk,rkl->rhl', weights.astype(jnp.float32), page_keys[:, :, :LAT].astype(jnp.float32))
    return context.astype(jnp.bfloat16)

def reference(kv_cache, queries, stream, page_table, lengths, send_pages, routes, value_up, output_weight, norm_gain, gate_weight, up_weight, down_weight):
    cache = kv_cache.reshape(N_AFD, PAGES_DEV, PAGE, LAT + ROPE)
    sends = send_pages.reshape(N_AFD, N_AFD, MIG)
    tables = page_table.reshape(N_AFD, TOK_DEV, MAXP)
    request_lengths = lengths.reshape(N_AFD, TOK_DEV)
    query = queries.reshape(N_AFD, TOK_DEV, H, LAT + ROPE)

    def one_device(device):
        return attend(cache, sends, tables[device], request_lengths[device], query[device], device)
    context = lax.map(one_device, jnp.arange(N_AFD, dtype=jnp.int32)).reshape(TOKENS, H, LAT)
    heads_out = jnp.einsum('thl,hlv->thv', context.astype(jnp.float32), value_up.astype(jnp.float32))
    heads_out = heads_out.astype(jnp.bfloat16).reshape(TOKENS, H * VDIM)
    hidden = (stream.astype(jnp.float32) + jnp.dot(heads_out, output_weight, preferred_element_type=jnp.float32)).astype(jnp.bfloat16)
    hidden_wide = hidden.astype(jnp.float32)
    normed = hidden_wide * lax.rsqrt(lax.optimization_barrier(jnp.mean(hidden_wide * hidden_wide, axis=-1, keepdims=True)) + norm_eps)
    normed = (normed * norm_gain.astype(jnp.float32)).astype(jnp.bfloat16)
    route = routes[:, 0].astype(jnp.int32)
    onehot = (route[:, None] == jnp.arange(EXPERTS, dtype=jnp.int32)[None, :]).astype(jnp.int32)
    rank = lax.optimization_barrier(jnp.sum((jnp.cumsum(onehot, axis=0) - onehot) * onehot, axis=1)).astype(jnp.int32)
    target = (route * CAP + rank).astype(jnp.int32)
    owner = jnp.full((EXPERTS * CAP,), TOKENS, jnp.int32).at[target].set(jnp.arange(TOKENS, dtype=jnp.int32))
    padded = jnp.concatenate([normed, jnp.zeros((1, D), jnp.bfloat16)], axis=0)
    buffer = padded[owner].reshape(EXPERTS, CAP, D)

    def expert_ffn(index):
        start = (index * FFH).astype(jnp.int32)
        gate_cols = lax.dynamic_slice_in_dim(gate_weight, start, FFH, 1)
        up_cols = lax.dynamic_slice_in_dim(up_weight, start, FFH, 1)
        down_rows = lax.dynamic_slice_in_dim(down_weight, start, FFH, 0)
        gate = jnp.dot(buffer[index], gate_cols, preferred_element_type=jnp.float32)
        up = jnp.dot(buffer[index], up_cols, preferred_element_type=jnp.float32)
        activated = (jax.nn.silu(gate) * up).astype(jnp.bfloat16)
        return jnp.dot(activated, down_rows, preferred_element_type=jnp.float32)
    expert_out = lax.map(expert_ffn, jnp.arange(EXPERTS, dtype=jnp.int32)).reshape(EXPERTS * CAP, D)
    return (hidden_wide + expert_out[target]).astype(jnp.bfloat16)
```

```python
import functools

import jax
import jax.numpy as jnp
from jax import lax
from jax.experimental import pallas as pl
from jax.experimental.pallas import tpu as pltpu
from jax.sharding import PartitionSpec as P

CAP = 240
MESH = pl.DeviceIdType.MESH
f32 = jnp.float32
bf16 = jnp.bfloat16

score_scale = 0.07216878364870322
norm_eps = 1e-06


def send(src, dst, send_sem, recv_sem, afd, tensor):
    return pltpu.make_async_remote_copy(
        src_ref=src,
        dst_ref=dst,
        send_sem=send_sem,
        recv_sem=recv_sem,
        device_id=(lax.axis_index("group"), afd, tensor),
        device_id_type=MESH,
    )


def greet(targets):
    barrier = pltpu.get_barrier_semaphore()
    for afd, tensor in targets:
        pl.semaphore_signal(
            barrier,
            inc=1,
            device_id=(lax.axis_index("group"), afd, tensor),
            device_id_type=MESH,
        )
    pl.semaphore_wait(barrier, len(targets))


def pages_kernel(count, out_ref, got_ref, sent_sem, got_sem, pass_sem, passed_sem, own_sem):
    me = lax.axis_index("afd")
    t = lax.axis_index("tensor")
    greet([(lax.rem(me + d, count), t) for d in range(1, count)] + [(me, 1 - t)])
    for d in range(1, count):
        to = lax.rem(me + d, count)
        send(out_ref.at[to], got_ref.at[me, t], sent_sem.at[to], got_sem.at[me], to, t).start()
    own = pltpu.make_async_copy(out_ref.at[me], got_ref.at[me, t], own_sem)
    own.start()
    own.wait()
    for d in range(count):
        src = lax.rem(me + count - d, count)
        if d > 0:
            send(out_ref.at[src], got_ref.at[src, t], sent_sem.at[src], got_sem.at[src], src, t).wait_recv()
        send(got_ref.at[src, t], got_ref.at[src, t], pass_sem.at[src], passed_sem.at[src], me, 1 - t).start()
    for d in range(count):
        src = lax.rem(me + count - d, count)
        back = send(got_ref.at[src, 1 - t], got_ref.at[src, 1 - t], pass_sem.at[src], passed_sem.at[src], me, 1 - t)
        back.wait_recv()
        back.wait_send()
    for d in range(1, count):
        to = lax.rem(me + d, count)
        send(out_ref.at[to], got_ref.at[me, t], sent_sem.at[to], got_sem.at[me], to, t).wait_send()


def exchange_pages(outgoing, count):
    dma = pltpu.SemaphoreType.DMA
    return pl.pallas_call(
        functools.partial(pages_kernel, count),
        out_shape=jax.ShapeDtypeStruct((count, 2) + outgoing.shape[1:], bf16),
        in_specs=[pl.BlockSpec(memory_space=pltpu.VMEM)],
        out_specs=pl.BlockSpec(memory_space=pltpu.VMEM),
        scratch_shapes=[dma((count,)), dma((count,)), dma((count,)), dma((count,)), dma],
        compiler_params=pltpu.CompilerParams(
            collective_id=0, has_side_effects=True, vmem_limit_bytes=40 * 2**20
        ),
    )(outgoing)


def project_kernel(
    pairs, heads_ref, w_hbm, stream_ref, hidden_ref,
    held, w, acc, half_out, half_in, w_sem, got_sem, up_sem, down_sem, side_sem, half_sems,
):
    me = lax.axis_index("afd")
    t = lax.axis_index("tensor")
    z, y = me // 2, lax.rem(me, 2)
    load = pltpu.make_async_copy(w_hbm, w, w_sem)
    load.start()
    greet(
        [(2 * lax.rem(z + d, pairs) + y, t) for d in range(1, pairs)]
        + [(2 * z + 1 - y, t), (me, 1 - t)]
    )
    held[me] = heads_ref[...]

    def side(slot):
        return send(held.at[slot], held.at[slot], side_sem.at[slot // 2], got_sem.at[slot], 2 * z + 1 - y, t)

    def up(slot):
        return send(held.at[slot], held.at[slot], up_sem.at[slot // 2], got_sem.at[slot], me + 2, t)

    def down(slot):
        return send(held.at[slot], held.at[slot], down_sem.at[slot // 2], got_sem.at[slot], me - 2, t)

    @pl.when(z + 1 < pairs)
    def _():
        up(me).start()

    @pl.when(z > 0)
    def _():
        down(me).start()

    side(me).start()
    for s in range(1, pairs):

        @pl.when(z - s >= 0)
        def _():
            slot = me - 2 * s
            up(slot).wait_recv()

            @pl.when(z + 1 < pairs)
            def _():
                up(slot).start()

            side(slot).start()

        @pl.when(z + s < pairs)
        def _():
            slot = me + 2 * s
            down(slot).wait_recv()

            @pl.when(z > 0)
            def _():
                down(slot).start()

            side(slot).start()

    for a in range(pairs):
        slot = 2 * a + 1 - y
        side(slot).wait_recv()
    for a in range(pairs):
        slot = 2 * a + y
        side(slot).wait_send()

        @pl.when((a <= z) & (z + 1 < pairs))
        def _():
            up(slot).wait_send()

        @pl.when((a >= z) & (z > 0))
        def _():
            down(slot).wait_send()

    load.wait()
    count, rows, depth = held.shape
    step = 512
    acc[...] = jnp.zeros_like(acc)

    def body(k, carry):
        at = pl.ds(pl.multiple_of(k * step, step), step)
        acc[...] += jnp.dot(
            held[:, :, at].reshape(count * rows, step), w[at, :], preferred_element_type=f32
        )
        return carry

    lax.fori_loop(0, depth // step, body, 0)
    width = half_out.shape[1]
    total = acc[...]
    left, right = total[:, :width], total[:, width:]
    first = t == 0
    half_out[...] = jnp.where(first, right, left)
    swap = send(half_out, half_in, half_sems.at[0], half_sems.at[1], me, 1 - t)
    swap.start()
    mine = jnp.where(first, left, right) + stream_ref[...].astype(f32)
    swap.wait()
    hidden_ref[...] = (mine + half_in[...]).astype(bf16)


def project(heads, weight, stream_half, pairs):
    dma = pltpu.SemaphoreType.DMA
    rows, depth = heads.shape
    tokens, width = stream_half.shape
    vmem = pl.BlockSpec(memory_space=pltpu.VMEM)
    return pl.pallas_call(
        functools.partial(project_kernel, pairs),
        out_shape=jax.ShapeDtypeStruct((tokens, width), bf16),
        in_specs=[vmem, pl.BlockSpec(memory_space=pl.ANY), vmem],
        out_specs=vmem,
        scratch_shapes=[
            pltpu.VMEM((2 * pairs, rows, depth), bf16),
            pltpu.VMEM(weight.shape, bf16),
            pltpu.VMEM((tokens, 2 * width), f32),
            pltpu.VMEM((tokens, width), f32),
            pltpu.VMEM((tokens, width), f32),
            dma,
            dma((2 * pairs,)),
            dma((pairs,)),
            dma((pairs,)),
            dma((pairs,)),
            dma((2,)),
        ],
        compiler_params=pltpu.CompilerParams(
            collective_id=1, has_side_effects=True, vmem_limit_bytes=48 * 2**20
        ),
    )(heads, weight, stream_half)


def experts_kernel(
    pairs, hidden_ref, pick_ref, place_ref, gain_ref, gate_hbm, up_hbm, down_hbm, out_ref,
    buf, rows, wg, wu, wd, acc_g, acc_u, squares, term1, send1, got1, send2, got2, send3, got3,
    w_sems, z_sem, row_sem, y_sem, t_sem, sems1, sems2, sems3,
):
    me = lax.axis_index("afd")
    t = lax.axis_index("tensor")
    z, y = me // 2, lax.rem(me, 2)
    beside = 2 * z + 1 - y
    width = hidden_ref.shape[1]
    loads = [
        pltpu.make_async_copy(a, b, w_sems.at[i])
        for i, (a, b) in enumerate(((gate_hbm, wg), (up_hbm, wu), (down_hbm, wd)))
    ]
    for load in loads:
        load.start()
    greet(
        [(2 * lax.rem(z + d, pairs) + y, t) for d in range(1, pairs)]
        + [(beside, t), (me, 1 - t)]
    )

    def along(e):
        return send(buf.at[e], rows.at[me, t], z_sem.at[e], row_sem.at[me, t], 2 * e + y, t)

    def across(slot):
        return send(rows.at[slot, t], rows.at[slot, t], y_sem.at[slot // 2], row_sem.at[slot, t], beside, t)

    def within(slot, side):
        return send(rows.at[slot, side], rows.at[slot, side], t_sem.at[slot], row_sem.at[slot, side], me, 1 - t)

    def build(d, carry):
        e = lax.rem(z + d, pairs)
        buf[e] = jnp.dot(pick_ref[e], hidden_ref[...], preferred_element_type=f32).astype(bf16)

        @pl.when(d < pairs)
        def _():
            along(e).start()

        return carry

    lax.fori_loop(1, pairs + 1, build, 0)
    rows[me, t] = buf[z]
    acc_g[...] = jnp.zeros_like(acc_g)
    acc_u[...] = jnp.zeros_like(acc_u)
    squares[...] = jnp.zeros_like(squares)
    loads[0].wait()
    loads[1].wait()

    def work(slot, side):
        block = slot * 2 + side
        wide = rows[slot, side].astype(f32)
        squares[...] += jnp.sum(wide * wide, axis=-1, keepdims=True)
        scaled = (wide * gain_ref[block]).astype(bf16)
        acc_g[...] += jnp.dot(scaled, wg[block], preferred_element_type=f32)
        acc_u[...] += jnp.dot(scaled, wu[block], preferred_element_type=f32)

    def straight(d, carry):
        slot = 2 * lax.rem(z + d, pairs) + y

        @pl.when(d > 0)
        def _():
            within(slot, t).wait_recv()

        across(slot).start()
        within(slot, t).start()
        work(slot, t)
        return carry

    lax.fori_loop(0, pairs, straight, 0)

    def sideways(d, carry):
        slot = 2 * lax.rem(z + d, pairs) + 1 - y
        within(slot, t).wait_recv()
        within(slot, t).start()
        work(slot, t)
        return carry

    lax.fori_loop(0, pairs, sideways, 0)

    def swapped(d, carry):
        for near in (True, False):
            slot = 2 * lax.rem(z + d, pairs) + (y if near else 1 - y)
            within(slot, 1 - t).wait_recv()
            work(slot, 1 - t)
        return carry

    lax.fori_loop(0, pairs, swapped, 0)
    depth = 2 * pairs * 2 * width
    scale = lax.rsqrt(squares[...] / depth + norm_eps)
    gate = acc_g[...] * scale
    activated = (jax.nn.silu(gate) * (acc_u[...] * scale)).astype(bf16)
    loads[2].wait()
    first = t == 0

    def swap1(a):
        return send(send1.at[a], got1.at[a], sems1.at[0, a], sems1.at[1, a], me, 1 - t)

    for a in range(2 * pairs):
        part = jnp.dot(
            activated, wd[:, a * 2 * width : (a + 1) * 2 * width], preferred_element_type=f32
        )
        left, right = part[:, :width], part[:, width:]
        send1[a] = jnp.where(first, right, left).astype(bf16)
        swap1(a).start()
        term1[a] = jnp.where(first, left, right)

    def swap2(e):
        return send(send2.at[e], got2.at[e], sems2.at[0, e], sems2.at[1, e], beside, t)

    def reduce2(d, carry):
        e = lax.rem(z + d, pairs)
        a = 2 * e + 1 - y
        swap1(a).wait_recv()
        send2[e] = (term1[a] + got1[a].astype(f32)).astype(bf16)
        swap2(e).start()
        return carry

    lax.fori_loop(1, pairs + 1, reduce2, 0)

    def give3(e):
        return send(send3.at[e], got3.at[z], sems3.at[0, e], sems3.at[1, z], 2 * e + y, t)

    def take3(e):
        return send(send3.at[e], got3.at[e], sems3.at[0, e], sems3.at[1, e], 2 * e + y, t)

    def reduce3(d, carry):
        e = lax.rem(z + d, pairs)
        a = 2 * e + y
        swap1(a).wait_recv()
        swap2(e).wait_recv()
        total = (term1[a] + got1[a].astype(f32) + got2[e].astype(f32)).astype(bf16)
        send3[e] = total

        @pl.when(d < pairs)
        def _():
            give3(e).start()

        return carry

    lax.fori_loop(1, pairs + 1, reduce3, 0)
    got3[z] = send3[z]
    mixed = hidden_ref[...].astype(f32)
    for d in range(pairs):
        e = lax.rem(z + d, pairs)
        if d > 0:
            take3(e).wait_recv()
        mixed += jnp.dot(place_ref[e], got3[e], preferred_element_type=f32)
    out_ref[...] = mixed.astype(bf16)
    for d in range(1, pairs):
        e = lax.rem(z + d, pairs)
        along(e).wait_send()
        give3(e).wait_send()
    for e in range(pairs):
        across(2 * e + y).wait_send()
        swap2(e).wait_send()
    for a in range(2 * pairs):
        within(a, t).wait_send()
        swap1(a).wait_send()


def run_experts(hidden, pick, place, gain, gate, up, down, pairs):
    dma = pltpu.SemaphoreType.DMA
    tokens, width = hidden.shape
    vmem = pl.BlockSpec(memory_space=pltpu.VMEM)
    hbm = pl.BlockSpec(memory_space=pl.ANY)
    count = 2 * pairs
    units = gate.shape[1]
    blocks = (2 * count, width, units)

    def tile(*lead):
        return pltpu.VMEM(lead + (CAP, width), bf16)

    return pl.pallas_call(
        functools.partial(experts_kernel, pairs),
        out_shape=jax.ShapeDtypeStruct((tokens, width), bf16),
        in_specs=[vmem, vmem, vmem, vmem, hbm, hbm, hbm],
        out_specs=vmem,
        scratch_shapes=[
            tile(pairs),
            tile(count, 2),
            pltpu.VMEM(blocks, bf16),
            pltpu.VMEM(blocks, bf16),
            pltpu.VMEM(down.shape, bf16),
            pltpu.VMEM((CAP, units), f32),
            pltpu.VMEM((CAP, units), f32),
            pltpu.VMEM((CAP, 1), f32),
            pltpu.VMEM((count, CAP, width), f32),
            tile(count),
            tile(count),
            tile(pairs),
            tile(pairs),
            tile(pairs),
            tile(pairs),
            dma((3,)),
            dma((pairs,)),
            dma((count, 2)),
            dma((pairs,)),
            dma((count,)),
            dma((2, count)),
            dma((2, pairs)),
            dma((2, pairs)),
        ],
        compiler_params=pltpu.CompilerParams(
            collective_id=2, has_side_effects=True, vmem_limit_bytes=56 * 2**20
        ),
    )(
        hidden, pick, place, gain.reshape(2 * count, 1, width),
        gate.reshape(blocks), up.reshape(blocks), down,
    )


def on_device(
    kv_cache,
    queries,
    stream,
    page_table,
    lengths,
    send_pages,
    routes,
    value_up,
    output_weight,
    norm_gain,
    gate_weight,
    up_weight,
    down_weight,
):
    afd_count = lax.axis_size("afd")
    pairs = afd_count // 2
    t = lax.axis_index("tensor")
    pages_dev, page_len, channels = kv_cache.shape
    requests, max_pages = page_table.shape
    migrate_count = send_pages.shape[1]
    moved_total = afd_count * migrate_count
    local_count = pages_dev - moved_total
    latent = value_up.shape[1]
    each = migrate_count // 2

    mine = lax.dynamic_slice_in_dim(send_pages, t * each, each, 1)
    moved = exchange_pages(kv_cache[mine], afd_count).reshape(moved_total, page_len, channels)

    slots = jnp.arange(pages_dev, dtype=jnp.int32)
    place = jnp.arange(max_pages, dtype=jnp.int32)
    used = place[None, :] * page_len < lengths[:, None]
    match = (page_table[:, :, None] == slots) & used[:, :, None]
    owns = jnp.any(match, axis=1)
    owner = jnp.sum(
        jnp.where(owns, jnp.arange(requests, dtype=jnp.int32)[:, None], 0), axis=0
    )
    left = lengths[:, None] - place[None, :] * page_len
    limit = jnp.sum(jnp.where(match, left[:, :, None], 0), axis=(0, 1))
    asked = queries[owner]

    def page_part(pages, lo, hi):
        scores = (
            jnp.einsum("shc,skc->shk", asked[lo:hi], pages, preferred_element_type=f32)
            * score_scale
        )
        position = jnp.arange(page_len, dtype=jnp.int32)
        scores = jnp.where(position[None, None, :] < limit[lo:hi, None, None], scores, -jnp.inf)
        highest = jnp.max(scores, axis=-1, keepdims=True)
        exponent = jnp.exp(scores - highest)
        total = jnp.sum(exponent, axis=-1)
        part = jnp.einsum(
            "shk,skl->shl", exponent.astype(bf16), pages[:, :, :latent], preferred_element_type=f32
        ).astype(bf16)
        return highest[:, :, 0], total, part

    m0, l0, o0 = page_part(kv_cache[:local_count], 0, local_count)
    m1, l1, o1 = page_part(moved, local_count, pages_dev)
    highest = jnp.concatenate([m0, m1], 0).T
    total = jnp.concatenate([l0, l1], 0).T
    part = jnp.concatenate([o0, o1], 0)
    own = owns[None, :, :]
    peak = jnp.max(jnp.where(own, highest[:, None, :], -jnp.inf), axis=-1, keepdims=True)
    factor = jnp.where(own, jnp.exp(jnp.where(own, highest[:, None, :] - peak, 0.0)), 0.0)
    mass = jnp.sum(factor * total[:, None, :], axis=-1, keepdims=True)
    share = (factor / mass).astype(bf16)
    context = jnp.einsum("hrs,shl->hrl", share, part, preferred_element_type=f32).astype(bf16)
    heads_out = jnp.einsum("hrl,hlv->rhv", context, value_up, preferred_element_type=f32)
    heads_out = heads_out.astype(bf16).reshape(requests, -1)

    width = stream.shape[1] // 2
    stream_half = lax.dynamic_slice_in_dim(stream, t * width, width, 1)
    hidden = project(heads_out, output_weight, stream_half, pairs)

    route = routes[:, 0]
    onehot = (route[:, None] == jnp.arange(pairs, dtype=jnp.int32)[None, :]).astype(jnp.int32)
    rank = jnp.sum((jnp.cumsum(onehot, axis=0) - onehot) * onehot, axis=1)
    seats = jnp.arange(CAP, dtype=jnp.int32)
    named = route[None, :] == jnp.arange(pairs, dtype=jnp.int32)[:, None]
    pick = ((rank[None, None, :] == seats[None, :, None]) & named[:, None, :]).astype(bf16)
    put = ((rank[None, :, None] == seats[None, None, :]) & named[:, :, None]).astype(bf16)
    return run_experts(hidden, pick, put, norm_gain, gate_weight, up_weight, down_weight, pairs)


def solution(mesh):
    in_specs = (
        P(("group", "afd"), None, None),
        P(("group", "afd"), "tensor", None),
        P("group", "afd"),
        P(("group", "afd"), None),
        P(("group", "afd")),
        P(("group", "afd"), None),
        P("group", None),
        P("tensor", None, None),
        P("tensor", "afd"),
        P(),
        P(None, ("afd", "tensor")),
        P(None, ("afd", "tensor")),
        P(("afd", "tensor"), None),
    )
    out_specs = P("group", ("afd", "tensor"))
    return jax.shard_map(
        on_device, mesh=mesh, in_specs=in_specs, out_specs=out_specs, check_vma=False
    )
```

```python
import functools

import jax
import jax.numpy as jnp
from jax import lax
from jax.experimental import pallas as pl
from jax.experimental.pallas import tpu as pltpu
from jax.sharding import PartitionSpec as P

CAP = 240
MESH = pl.DeviceIdType.MESH
f32 = jnp.float32
bf16 = jnp.bfloat16

score_scale = 0.07216878364870322
norm_eps = 1e-06


def send(src, dst, send_sem, recv_sem, afd, tensor):
    return pltpu.make_async_remote_copy(
        src_ref=src,
        dst_ref=dst,
        send_sem=send_sem,
        recv_sem=recv_sem,
        device_id=(lax.axis_index("group"), afd, tensor),
        device_id_type=MESH,
    )


def greet(targets):
    barrier = pltpu.get_barrier_semaphore()
    for afd, tensor in targets:
        pl.semaphore_signal(
            barrier,
            inc=1,
            device_id=(lax.axis_index("group"), afd, tensor),
            device_id_type=MESH,
        )
    pl.semaphore_wait(barrier, len(targets))


def attend_kernel(
    count, each, local, owner_ref, limit_ref, give_ref, kv_ref, q_ref, part_ref, top_ref, mass_ref,
    out, got, sent_sem, got_sem, pass_sem, passed_sem,
):
    me = lax.axis_index("afd")
    t = lax.axis_index("tensor")
    greet([(lax.rem(me + d, count), t) for d in range(1, count)] + [(me, 1 - t)])
    latent = part_ref.shape[2]

    def page_to(to):
        return send(out.at[to], got.at[me, t], sent_sem.at[to], got_sem.at[me], to, t)

    def page_from(src):
        return send(out.at[src], got.at[src, t], sent_sem.at[src], got_sem.at[src], src, t)

    def swap(src, side):
        return send(got.at[src, side], got.at[src, side], pass_sem.at[src], passed_sem.at[src], me, 1 - t)

    for d in range(1, count):
        to = lax.rem(me + d, count)
        for j in range(each):
            out[to, j] = kv_ref[give_ref[to * each + j]]
        page_to(to).start()
    for j in range(each):
        got[me, t, j] = kv_ref[give_ref[me * each + j]]
    swap(me, t).start()

    def one(slot, page):
        scores = lax.dot_general(
            page, q_ref[owner_ref[slot]], (((1,), (1,)), ((), ())), preferred_element_type=f32
        ) * score_scale
        position = lax.broadcasted_iota(jnp.int32, scores.shape, 0)
        scores = jnp.where(position < limit_ref[slot], scores, -jnp.inf)
        top = jnp.max(scores, axis=0, keepdims=True)
        exponent = jnp.exp(scores - top)
        top_ref[slot] = top
        mass_ref[slot] = jnp.sum(exponent, axis=0, keepdims=True)
        part_ref[slot] = lax.dot_general(
            exponent.astype(bf16), page[:, :latent], (((0,), (0,)), ((), ())),
            preferred_element_type=f32,
        ).astype(bf16)

    def forward(d):
        src = lax.rem(me + d, count)
        page_from(src).wait_recv()
        swap(src, t).start()

    pace = local // count

    def resident(i, carry):
        for j in range(pace):
            one(i * pace + j, kv_ref[i * pace + j])
        return carry

    def resident_and_forward(i, carry):
        resident(i, carry)
        forward(i)
        return carry

    resident(0, 0)
    lax.fori_loop(1, count, resident_and_forward, 0)
    for slot in range(pace * count, local):
        one(slot, kv_ref[slot])

    def arrived(d, carry):
        src = lax.rem(me + d, count)
        swap(src, 1 - t).wait_recv()
        for side in range(2):
            for j in range(each):
                one(local + (src * 2 + side) * each + j, got[src, side, j])
        return carry

    lax.fori_loop(0, count, arrived, 0)
    for d in range(count):
        to = lax.rem(me + d, count)
        swap(to, t).wait_send()
        if d > 0:
            page_to(to).wait_send()


def attend(kv_cache, queries, owner, limit, give, count, each, local, latent):
    dma = pltpu.SemaphoreType.DMA
    slots, page_len, channels = kv_cache.shape
    heads = queries.shape[1]
    vmem = pl.BlockSpec(memory_space=pltpu.VMEM)
    smem = pl.BlockSpec(memory_space=pltpu.SMEM)
    return pl.pallas_call(
        functools.partial(attend_kernel, count, each, local),
        out_shape=(
            jax.ShapeDtypeStruct((slots, heads, latent), bf16),
            jax.ShapeDtypeStruct((slots, 1, heads), f32),
            jax.ShapeDtypeStruct((slots, 1, heads), f32),
        ),
        in_specs=[smem, smem, smem, vmem, vmem],
        out_specs=(vmem, vmem, vmem),
        scratch_shapes=[
            pltpu.VMEM((count, each, page_len, channels), bf16),
            pltpu.VMEM((count, 2, each, page_len, channels), bf16),
            dma((count,)), dma((count,)), dma((count,)), dma((count,)),
        ],
        compiler_params=pltpu.CompilerParams(
            collective_id=0, has_side_effects=True, vmem_limit_bytes=40 * 2**20
        ),
    )(owner, limit, give, kv_cache, queries)


def project_kernel(
    pairs, heads_ref, w_hbm, stream_ref, hidden_ref,
    held, w, acc, half_out, half_in, w_sem, got_sem, up_sem, down_sem, side_sem, half_sems,
):
    me = lax.axis_index("afd")
    t = lax.axis_index("tensor")
    z, y = me // 2, lax.rem(me, 2)
    load = pltpu.make_async_copy(w_hbm, w, w_sem)
    load.start()
    greet(
        [(2 * lax.rem(z + d, pairs) + y, t) for d in range(1, pairs)]
        + [(2 * z + 1 - y, t), (me, 1 - t)]
    )
    chunks, count, rows, step = held.shape

    def side(c, slot):
        here = held.at[c, slot]
        return send(here, here, side_sem.at[c, slot // 2], got_sem.at[c, slot], 2 * z + 1 - y, t)

    def up(c, slot):
        here = held.at[c, slot]
        return send(here, here, up_sem.at[c, slot // 2], got_sem.at[c, slot], me + 2, t)

    def down(c, slot):
        here = held.at[c, slot]
        return send(here, here, down_sem.at[c, slot // 2], got_sem.at[c, slot], me - 2, t)

    def begin(c):
        held[c, me] = heads_ref[:, c * step : (c + 1) * step]

        @pl.when(z + 1 < pairs)
        def _():
            up(c, me).start()

        @pl.when(z > 0)
        def _():
            down(c, me).start()

        side(c, me).start()

    def relay(c, s):
        @pl.when(z - s >= 0)
        def _():
            slot = me - 2 * s
            up(c, slot).wait_recv()

            @pl.when(z + 1 < pairs)
            def _():
                up(c, slot).start()

            side(c, slot).start()

        @pl.when(z + s < pairs)
        def _():
            slot = me + 2 * s
            down(c, slot).wait_recv()

            @pl.when(z > 0)
            def _():
                down(c, slot).start()

            side(c, slot).start()

    def finish(c):
        for a in range(pairs):
            side(c, 2 * a + 1 - y).wait_recv()
        block = held[c].reshape(count * rows, step)
        acc[...] += jnp.dot(block, w[c * step : (c + 1) * step, :], preferred_element_type=f32)

    acc[...] = jnp.zeros_like(acc)
    for turn in range(chunks + pairs):
        if turn < chunks:
            begin(turn)
        for s in range(pairs - 1, 0, -1):
            if 0 <= turn - s < chunks:
                relay(turn - s, s)
        if turn == pairs:
            load.wait()
        if turn >= pairs:
            finish(turn - pairs)
    for c in range(chunks):
        for a in range(pairs):
            slot = 2 * a + y
            side(c, slot).wait_send()

            @pl.when((a <= z) & (z + 1 < pairs))
            def _():
                up(c, slot).wait_send()

            @pl.when((a >= z) & (z > 0))
            def _():
                down(c, slot).wait_send()

    width = half_out.shape[1]
    total = acc[...]
    left, right = total[:, :width], total[:, width:]
    first = t == 0
    half_out[...] = jnp.where(first, right, left)
    swap = send(half_out, half_in, half_sems.at[0], half_sems.at[1], me, 1 - t)
    swap.start()
    mine = jnp.where(first, left, right) + stream_ref[...].astype(f32)
    swap.wait()
    hidden_ref[...] = (mine + half_in[...]).astype(bf16)


def project(heads, weight, stream_half, pairs):
    dma = pltpu.SemaphoreType.DMA
    rows, depth = heads.shape
    tokens, width = stream_half.shape
    chunks = 4
    vmem = pl.BlockSpec(memory_space=pltpu.VMEM)
    return pl.pallas_call(
        functools.partial(project_kernel, pairs),
        out_shape=jax.ShapeDtypeStruct((tokens, width), bf16),
        in_specs=[vmem, pl.BlockSpec(memory_space=pl.ANY), vmem],
        out_specs=vmem,
        scratch_shapes=[
            pltpu.VMEM((chunks, 2 * pairs, rows, depth // chunks), bf16),
            pltpu.VMEM(weight.shape, bf16),
            pltpu.VMEM((tokens, 2 * width), f32),
            pltpu.VMEM((tokens, width), f32),
            pltpu.VMEM((tokens, width), f32),
            dma,
            dma((chunks, 2 * pairs)),
            dma((chunks, pairs)),
            dma((chunks, pairs)),
            dma((chunks, pairs)),
            dma((2,)),
        ],
        compiler_params=pltpu.CompilerParams(
            collective_id=1, has_side_effects=True, vmem_limit_bytes=48 * 2**20
        ),
    )(heads, weight, stream_half)


def experts_kernel(
    pairs, hidden_ref, pick_ref, place_ref, gain_ref, gate_hbm, up_hbm, down_hbm, out_ref,
    buf, rows, wg, wu, wd, acc_g, acc_u, squares, term1, send1, got1, send2, got2, send3, got3,
    w_sems, z_sem, row_sem, y_sem, t_sem, sems1, sems2, sems3,
):
    me = lax.axis_index("afd")
    t = lax.axis_index("tensor")
    z, y = me // 2, lax.rem(me, 2)
    beside = 2 * z + 1 - y
    width = hidden_ref.shape[1]
    loads = [
        pltpu.make_async_copy(a, b, w_sems.at[i])
        for i, (a, b) in enumerate(((gate_hbm, wg), (up_hbm, wu), (down_hbm, wd)))
    ]
    for load in loads:
        load.start()
    greet(
        [(2 * lax.rem(z + d, pairs) + y, t) for d in range(1, pairs)]
        + [(beside, t), (me, 1 - t)]
    )

    def along(e):
        return send(buf.at[e], rows.at[me, t], z_sem.at[e], row_sem.at[me, t], 2 * e + y, t)

    def across(slot):
        return send(rows.at[slot, t], rows.at[slot, t], y_sem.at[slot // 2], row_sem.at[slot, t], beside, t)

    def within(slot, side):
        return send(rows.at[slot, side], rows.at[slot, side], t_sem.at[slot], row_sem.at[slot, side], me, 1 - t)

    def build(d, carry):
        e = lax.rem(z + d, pairs)
        buf[e] = jnp.dot(pick_ref[e], hidden_ref[...], preferred_element_type=f32).astype(bf16)

        @pl.when(d < pairs)
        def _():
            along(e).start()

        return carry

    lax.fori_loop(1, pairs + 1, build, 0)
    rows[me, t] = buf[z]
    acc_g[...] = jnp.zeros_like(acc_g)
    acc_u[...] = jnp.zeros_like(acc_u)
    squares[...] = jnp.zeros_like(squares)
    loads[0].wait()
    loads[1].wait()

    def work(slot, side):
        block = slot * 2 + side
        wide = rows[slot, side].astype(f32)
        squares[...] += jnp.sum(wide * wide, axis=-1, keepdims=True)
        scaled = (wide * gain_ref[block]).astype(bf16)
        acc_g[...] += jnp.dot(scaled, wg[block], preferred_element_type=f32)
        acc_u[...] += jnp.dot(scaled, wu[block], preferred_element_type=f32)

    def straight(d, carry):
        slot = 2 * lax.rem(z + d, pairs) + y

        @pl.when(d > 0)
        def _():
            within(slot, t).wait_recv()

        across(slot).start()
        within(slot, t).start()
        work(slot, t)
        return carry

    lax.fori_loop(0, pairs, straight, 0)

    def sideways(d, carry):
        slot = 2 * lax.rem(z + d, pairs) + 1 - y
        within(slot, t).wait_recv()
        within(slot, t).start()
        work(slot, t)
        return carry

    lax.fori_loop(0, pairs, sideways, 0)

    def swapped(d, carry):
        for near in (True, False):
            slot = 2 * lax.rem(z + d, pairs) + (y if near else 1 - y)
            within(slot, 1 - t).wait_recv()
            work(slot, 1 - t)
        return carry

    lax.fori_loop(0, pairs, swapped, 0)
    depth = 2 * pairs * 2 * width
    scale = lax.rsqrt(squares[...] / depth + norm_eps)
    gate = acc_g[...] * scale
    activated = (jax.nn.silu(gate) * (acc_u[...] * scale)).astype(bf16)
    loads[2].wait()
    first = t == 0

    def swap1(a):
        return send(send1.at[a], got1.at[a], sems1.at[0, a], sems1.at[1, a], me, 1 - t)

    for a in range(2 * pairs):
        part = jnp.dot(
            activated, wd[:, a * 2 * width : (a + 1) * 2 * width], preferred_element_type=f32
        )
        left, right = part[:, :width], part[:, width:]
        send1[a] = jnp.where(first, right, left).astype(bf16)
        swap1(a).start()
        term1[a] = jnp.where(first, left, right)

    def swap2(e):
        return send(send2.at[e], got2.at[e], sems2.at[0, e], sems2.at[1, e], beside, t)

    def reduce2(d, carry):
        e = lax.rem(z + d, pairs)
        a = 2 * e + 1 - y
        swap1(a).wait_recv()
        send2[e] = (term1[a] + got1[a].astype(f32)).astype(bf16)
        swap2(e).start()
        return carry

    lax.fori_loop(1, pairs + 1, reduce2, 0)

    def give3(e):
        return send(send3.at[e], got3.at[z], sems3.at[0, e], sems3.at[1, z], 2 * e + y, t)

    def take3(e):
        return send(send3.at[e], got3.at[e], sems3.at[0, e], sems3.at[1, e], 2 * e + y, t)

    def reduce3(d, carry):
        e = lax.rem(z + d, pairs)
        a = 2 * e + y
        swap1(a).wait_recv()
        swap2(e).wait_recv()
        total = (term1[a] + got1[a].astype(f32) + got2[e].astype(f32)).astype(bf16)
        send3[e] = total

        @pl.when(d < pairs)
        def _():
            give3(e).start()

        return carry

    lax.fori_loop(1, pairs + 1, reduce3, 0)
    got3[z] = send3[z]
    mixed = hidden_ref[...].astype(f32)
    for d in range(pairs):
        e = lax.rem(z + d, pairs)
        if d > 0:
            take3(e).wait_recv()
        mixed += jnp.dot(place_ref[e], got3[e], preferred_element_type=f32)
    out_ref[...] = mixed.astype(bf16)
    for d in range(1, pairs):
        e = lax.rem(z + d, pairs)
        along(e).wait_send()
        give3(e).wait_send()
    for e in range(pairs):
        across(2 * e + y).wait_send()
        swap2(e).wait_send()
    for a in range(2 * pairs):
        within(a, t).wait_send()
        swap1(a).wait_send()


def run_experts(hidden, pick, place, gain, gate, up, down, pairs):
    dma = pltpu.SemaphoreType.DMA
    tokens, width = hidden.shape
    vmem = pl.BlockSpec(memory_space=pltpu.VMEM)
    hbm = pl.BlockSpec(memory_space=pl.ANY)
    count = 2 * pairs
    units = gate.shape[1]
    blocks = (2 * count, width, units)

    def tile(*lead):
        return pltpu.VMEM(lead + (CAP, width), bf16)

    return pl.pallas_call(
        functools.partial(experts_kernel, pairs),
        out_shape=jax.ShapeDtypeStruct((tokens, width), bf16),
        in_specs=[vmem, vmem, vmem, vmem, hbm, hbm, hbm],
        out_specs=vmem,
        scratch_shapes=[
            tile(pairs),
            tile(count, 2),
            pltpu.VMEM(blocks, bf16),
            pltpu.VMEM(blocks, bf16),
            pltpu.VMEM(down.shape, bf16),
            pltpu.VMEM((CAP, units), f32),
            pltpu.VMEM((CAP, units), f32),
            pltpu.VMEM((CAP, 1), f32),
            pltpu.VMEM((count, CAP, width), f32),
            tile(count),
            tile(count),
            tile(pairs),
            tile(pairs),
            tile(pairs),
            tile(pairs),
            dma((3,)),
            dma((pairs,)),
            dma((count, 2)),
            dma((pairs,)),
            dma((count,)),
            dma((2, count)),
            dma((2, pairs)),
            dma((2, pairs)),
        ],
        compiler_params=pltpu.CompilerParams(
            collective_id=2, has_side_effects=True, vmem_limit_bytes=56 * 2**20
        ),
    )(
        hidden, pick, place, gain.reshape(2 * count, 1, width),
        gate.reshape(blocks), up.reshape(blocks), down,
    )


def on_device(
    kv_cache,
    queries,
    stream,
    page_table,
    lengths,
    send_pages,
    routes,
    value_up,
    output_weight,
    norm_gain,
    gate_weight,
    up_weight,
    down_weight,
):
    afd_count = lax.axis_size("afd")
    pairs = afd_count // 2
    t = lax.axis_index("tensor")
    pages_dev, page_len, channels = kv_cache.shape
    requests, max_pages = page_table.shape
    migrate_count = send_pages.shape[1]
    moved_total = afd_count * migrate_count
    local_count = pages_dev - moved_total
    latent = value_up.shape[1]
    each = migrate_count // 2

    give = lax.dynamic_slice_in_dim(send_pages, t * each, each, 1).reshape(-1)

    slots = jnp.arange(pages_dev, dtype=jnp.int32)
    place = jnp.arange(max_pages, dtype=jnp.int32)
    used = place[None, :] * page_len < lengths[:, None]
    match = (page_table[:, :, None] == slots) & used[:, :, None]
    owns = jnp.any(match, axis=1)
    owner = jnp.sum(
        jnp.where(owns, jnp.arange(requests, dtype=jnp.int32)[:, None], 0), axis=0
    )
    left = lengths[:, None] - place[None, :] * page_len
    limit = jnp.sum(jnp.where(match, left[:, :, None], 0), axis=(0, 1))
    part, highest, total = attend(
        kv_cache, queries, owner, limit, give, afd_count, each, local_count, latent
    )
    highest = highest[:, 0].T
    total = total[:, 0].T
    own = owns[None, :, :]
    peak = jnp.max(jnp.where(own, highest[:, None, :], -jnp.inf), axis=-1, keepdims=True)
    factor = jnp.where(own, jnp.exp(jnp.where(own, highest[:, None, :] - peak, 0.0)), 0.0)
    mass = jnp.sum(factor * total[:, None, :], axis=-1, keepdims=True)
    share = (factor / mass).astype(bf16)
    context = jnp.einsum("hrs,shl->hrl", share, part, preferred_element_type=f32).astype(bf16)
    heads_out = jnp.einsum("hrl,hlv->rhv", context, value_up, preferred_element_type=f32)
    heads_out = heads_out.astype(bf16).reshape(requests, -1)

    width = stream.shape[1] // 2
    stream_half = lax.dynamic_slice_in_dim(stream, t * width, width, 1)
    hidden = project(heads_out, output_weight, stream_half, pairs)

    route = routes[:, 0]
    onehot = (route[:, None] == jnp.arange(pairs, dtype=jnp.int32)[None, :]).astype(jnp.int32)
    rank = jnp.sum((jnp.cumsum(onehot, axis=0) - onehot) * onehot, axis=1)
    seats = jnp.arange(CAP, dtype=jnp.int32)
    named = route[None, :] == jnp.arange(pairs, dtype=jnp.int32)[:, None]
    pick = ((rank[None, None, :] == seats[None, :, None]) & named[:, None, :]).astype(bf16)
    put = ((rank[None, :, None] == seats[None, None, :]) & named[:, :, None]).astype(bf16)
    return run_experts(hidden, pick, put, norm_gain, gate_weight, up_weight, down_weight, pairs)


def solution(mesh):
    in_specs = (
        P(("group", "afd"), None, None),
        P(("group", "afd"), "tensor", None),
        P("group", "afd"),
        P(("group", "afd"), None),
        P(("group", "afd")),
        P(("group", "afd"), None),
        P("group", None),
        P("tensor", None, None),
        P("tensor", "afd"),
        P(),
        P(None, ("afd", "tensor")),
        P(None, ("afd", "tensor")),
        P(("afd", "tensor"), None),
    )
    out_specs = P("group", ("afd", "tensor"))
    return jax.shard_map(
        on_device, mesh=mesh, in_specs=in_specs, out_specs=out_specs, check_vma=False
    )
```

```python
import functools

import jax
import jax.numpy as jnp
from jax import lax
from jax.experimental import pallas as pl
from jax.experimental.pallas import tpu as pltpu
from jax.sharding import PartitionSpec as P

CAP = 240
MESH = pl.DeviceIdType.MESH
f32 = jnp.float32
bf16 = jnp.bfloat16

score_scale = 0.07216878364870322
norm_eps = 1e-06


def send(src, dst, send_sem, recv_sem, afd, tensor):
    return pltpu.make_async_remote_copy(
        src_ref=src,
        dst_ref=dst,
        send_sem=send_sem,
        recv_sem=recv_sem,
        device_id=(lax.axis_index("group"), afd, tensor),
        device_id_type=MESH,
    )


def greet(targets):
    barrier = pltpu.get_barrier_semaphore()
    for afd, tensor in targets:
        pl.semaphore_signal(
            barrier,
            inc=1,
            device_id=(lax.axis_index("group"), afd, tensor),
            device_id_type=MESH,
        )
    pl.semaphore_wait(barrier, len(targets))


def attend_kernel(
    count, each, local, owner_ref, limit_ref, give_ref, kv_ref, q_ref, part_ref, top_ref, mass_ref,
    out, got, sent_sem, got_sem, pass_sem, passed_sem,
):
    me = lax.axis_index("afd")
    t = lax.axis_index("tensor")
    greet([(lax.rem(me + d, count), t) for d in range(1, count)] + [(me, 1 - t)])
    latent = part_ref.shape[2]

    def page_to(to):
        return send(out.at[to], got.at[me, t], sent_sem.at[to], got_sem.at[me], to, t)

    def page_from(src):
        return send(out.at[src], got.at[src, t], sent_sem.at[src], got_sem.at[src], src, t)

    def swap(src, side):
        return send(got.at[src, side], got.at[src, side], pass_sem.at[src], passed_sem.at[src], me, 1 - t)

    for d in range(1, count):
        to = lax.rem(me + d, count)
        for j in range(each):
            out[to, j] = kv_ref[give_ref[to * each + j]]
        page_to(to).start()
    for j in range(each):
        got[me, t, j] = kv_ref[give_ref[me * each + j]]
    swap(me, t).start()

    def one(slot, page):
        scores = lax.dot_general(
            page, q_ref[owner_ref[slot]], (((1,), (1,)), ((), ())), preferred_element_type=f32
        ) * score_scale
        position = lax.broadcasted_iota(jnp.int32, scores.shape, 0)
        scores = jnp.where(position < limit_ref[slot], scores, -jnp.inf)
        top = jnp.max(scores, axis=0, keepdims=True)
        exponent = jnp.exp(scores - top)
        top_ref[slot] = top
        mass_ref[slot] = jnp.sum(exponent, axis=0, keepdims=True)
        part_ref[slot] = lax.dot_general(
            exponent.astype(bf16), page[:, :latent], (((0,), (0,)), ((), ())),
            preferred_element_type=f32,
        ).astype(bf16)

    def forward(d):
        src = lax.rem(me + d, count)
        page_from(src).wait_recv()
        swap(src, t).start()

    pace = local // count

    def resident(i, carry):
        for j in range(pace):
            one(i * pace + j, kv_ref[i * pace + j])
        return carry

    def resident_and_forward(i, carry):
        resident(i, carry)
        forward(i)
        return carry

    resident(0, 0)
    lax.fori_loop(1, count, resident_and_forward, 0)
    for slot in range(pace * count, local):
        one(slot, kv_ref[slot])

    def arrived(d, carry):
        src = lax.rem(me + d, count)
        swap(src, 1 - t).wait_recv()
        for side in range(2):
            for j in range(each):
                one(local + (src * 2 + side) * each + j, got[src, side, j])
        return carry

    lax.fori_loop(0, count, arrived, 0)
    for d in range(count):
        to = lax.rem(me + d, count)
        swap(to, t).wait_send()
        if d > 0:
            page_to(to).wait_send()


def attend(kv_cache, queries, owner, limit, give, count, each, local, latent):
    dma = pltpu.SemaphoreType.DMA
    slots, page_len, channels = kv_cache.shape
    heads = queries.shape[1]
    vmem = pl.BlockSpec(memory_space=pltpu.VMEM)
    smem = pl.BlockSpec(memory_space=pltpu.SMEM)
    return pl.pallas_call(
        functools.partial(attend_kernel, count, each, local),
        out_shape=(
            jax.ShapeDtypeStruct((slots, heads, latent), bf16),
            jax.ShapeDtypeStruct((slots, 1, heads), f32),
            jax.ShapeDtypeStruct((slots, 1, heads), f32),
        ),
        in_specs=[smem, smem, smem, vmem, vmem],
        out_specs=(vmem, vmem, vmem),
        scratch_shapes=[
            pltpu.VMEM((count, each, page_len, channels), bf16),
            pltpu.VMEM((count, 2, each, page_len, channels), bf16),
            dma((count,)), dma((count,)), dma((count,)), dma((count,)),
        ],
        compiler_params=pltpu.CompilerParams(
            collective_id=0, has_side_effects=True, vmem_limit_bytes=40 * 2**20
        ),
    )(owner, limit, give, kv_cache, queries)


def project_kernel(
    pairs, heads_ref, w_hbm, stream_ref, hidden_ref,
    held, w, acc, half_out, half_in, w_sem, got_sem, up_sem, down_sem, side_sem, cross_sem, half_sems,
):
    me = lax.axis_index("afd")
    t = lax.axis_index("tensor")
    z, y = me // 2, lax.rem(me, 2)
    load = pltpu.make_async_copy(w_hbm, w, w_sem)
    load.start()
    greet(
        [(2 * lax.rem(z + d, pairs) + y, t) for d in range(1, pairs)]
        + [(2 * z + 1 - y, t), (me, 1 - t)]
    )
    chunks, count, rows, step = held.shape

    def side(c, slot):
        here = held.at[c, slot]
        return send(here, here, side_sem.at[c, slot // 2], got_sem.at[c, slot], 2 * z + 1 - y, t)

    def up(c, slot):
        here = held.at[c, slot]
        return send(here, here, up_sem.at[c, slot // 2], got_sem.at[c, slot], me + 2, t)

    def down(c, slot):
        here = held.at[c, slot]
        return send(here, here, down_sem.at[c, slot // 2], got_sem.at[c, slot], me - 2, t)

    def begin(c):
        held[c, me] = heads_ref[:, c * step : (c + 1) * step]

        @pl.when(z + 1 < pairs)
        def _():
            up(c, me).start()

        @pl.when(z > 0)
        def _():
            down(c, me).start()

        side(c, me).start()

    mate = z + 1 - 2 * lax.rem(z, 2)

    def cross(c):
        here = held.at[c, 2 * z + 1 - y]
        return send(here, here, cross_sem.at[c], got_sem.at[c, 2 * z + 1 - y], 2 * mate + y, t)

    def crosses(c):
        return c % 2 == 1

    def beside(c, slot):
        if crosses(c):

            @pl.when(slot // 2 != mate)
            def _():
                side(c, slot).start()

        else:
            side(c, slot).start()

    def relay(c, s):
        if s == 1 and crosses(c):
            side(c, 2 * z + 1 - y).wait_recv()
            cross(c).start()

        @pl.when(z - s >= 0)
        def _():
            slot = me - 2 * s
            up(c, slot).wait_recv()

            @pl.when(z + 1 < pairs)
            def _():
                up(c, slot).start()

            beside(c, slot)

        @pl.when(z + s < pairs)
        def _():
            slot = me + 2 * s
            down(c, slot).wait_recv()

            @pl.when(z > 0)
            def _():
                down(c, slot).start()

            beside(c, slot)

    def finish(c):
        for a in range(pairs):
            if crosses(c):

                @pl.when(a != z)
                def _():
                    side(c, 2 * a + 1 - y).wait_recv()

            else:
                side(c, 2 * a + 1 - y).wait_recv()
        block = held[c].reshape(count * rows, step)
        acc[...] += jnp.dot(block, w[c * step : (c + 1) * step, :], preferred_element_type=f32)

    acc[...] = jnp.zeros_like(acc)
    for turn in range(chunks + pairs):
        if turn < chunks:
            begin(turn)
        for s in range(pairs - 1, 0, -1):
            if 0 <= turn - s < chunks:
                relay(turn - s, s)
        if turn == pairs:
            load.wait()
        if turn >= pairs:
            finish(turn - pairs)
    for c in range(chunks):
        if crosses(c):
            cross(c).wait_send()
        for a in range(pairs):
            slot = 2 * a + y
            if crosses(c):

                @pl.when(a != mate)
                def _():
                    side(c, slot).wait_send()

            else:
                side(c, slot).wait_send()

            @pl.when((a <= z) & (z + 1 < pairs))
            def _():
                up(c, slot).wait_send()

            @pl.when((a >= z) & (z > 0))
            def _():
                down(c, slot).wait_send()

    width = half_out.shape[1]
    total = acc[...]
    left, right = total[:, :width], total[:, width:]
    first = t == 0
    half_out[...] = jnp.where(first, right, left)
    swap = send(half_out, half_in, half_sems.at[0], half_sems.at[1], me, 1 - t)
    swap.start()
    mine = jnp.where(first, left, right) + stream_ref[...].astype(f32)
    swap.wait()
    hidden_ref[...] = (mine + half_in[...]).astype(bf16)


def project(heads, weight, stream_half, pairs):
    dma = pltpu.SemaphoreType.DMA
    rows, depth = heads.shape
    tokens, width = stream_half.shape
    chunks = 4
    vmem = pl.BlockSpec(memory_space=pltpu.VMEM)
    return pl.pallas_call(
        functools.partial(project_kernel, pairs),
        out_shape=jax.ShapeDtypeStruct((tokens, width), bf16),
        in_specs=[vmem, pl.BlockSpec(memory_space=pl.ANY), vmem],
        out_specs=vmem,
        scratch_shapes=[
            pltpu.VMEM((chunks, 2 * pairs, rows, depth // chunks), bf16),
            pltpu.VMEM(weight.shape, bf16),
            pltpu.VMEM((tokens, 2 * width), f32),
            pltpu.VMEM((tokens, width), f32),
            pltpu.VMEM((tokens, width), f32),
            dma,
            dma((chunks, 2 * pairs)),
            dma((chunks, pairs)),
            dma((chunks, pairs)),
            dma((chunks, pairs)),
            dma((chunks,)),
            dma((2,)),
        ],
        compiler_params=pltpu.CompilerParams(
            collective_id=1, has_side_effects=True, vmem_limit_bytes=48 * 2**20
        ),
    )(heads, weight, stream_half)


def experts_kernel(
    pairs, hidden_ref, target_row_ref, target_col_ref, gain_ref, gate_hbm, up_hbm, down_hbm, out_ref,
    buf, rows, wg, wu, wd, acc_g, acc_u, squares, term1, send1, got1, send2, got2, send3, got3,
    w_sems, z_sem, row_sem, y_sem, t_sem, sems1, sems2, sems3,
):
    me = lax.axis_index("afd")
    t = lax.axis_index("tensor")
    z, y = me // 2, lax.rem(me, 2)
    beside = 2 * z + 1 - y
    width = hidden_ref.shape[1]
    loads = [
        pltpu.make_async_copy(a, b, w_sems.at[i])
        for i, (a, b) in enumerate(((gate_hbm, wg), (up_hbm, wu), (down_hbm, wd)))
    ]
    for load in loads:
        load.start()
    greet(
        [(2 * lax.rem(z + d, pairs) + y, t) for d in range(1, pairs)]
        + [(beside, t), (me, 1 - t)]
    )

    halves = ((0, 128), (128, CAP - 128))

    def along(h, e):
        at = pl.ds(*halves[h])
        return send(buf.at[e, at], rows.at[me, t, at], z_sem.at[h, e], row_sem.at[h, me, t], 2 * e + y, t)

    def across(h, slot):
        here = rows.at[slot, t, pl.ds(*halves[h])]
        return send(here, here, y_sem.at[h, slot // 2], row_sem.at[h, slot, t], beside, t)

    def within(h, slot, side):
        here = rows.at[slot, side, pl.ds(*halves[h])]
        return send(here, here, t_sem.at[h, slot], row_sem.at[h, slot, side], me, 1 - t)

    def build(d, carry):
        e = lax.rem(z + d, pairs)
        seats = lax.broadcasted_iota(jnp.int32, (CAP, target_row_ref.shape[1]), 0) + e * CAP
        pick = jnp.where(seats == target_row_ref[...], 1.0, 0.0).astype(bf16)
        buf[e] = jnp.dot(pick, hidden_ref[...], preferred_element_type=f32).astype(bf16)

        @pl.when(d < pairs)
        def _():
            along(0, e).start()

        return carry

    lax.fori_loop(1, pairs + 1, build, 0)
    rows[me, t] = buf[z]
    for h in range(2):
        across(h, me).start()
        within(h, me, t).start()
    acc_g[...] = jnp.zeros_like(acc_g)
    acc_u[...] = jnp.zeros_like(acc_u)
    squares[...] = jnp.zeros_like(squares)
    loads[0].wait()
    loads[1].wait()

    def work(h, slot, side):
        block = slot * 2 + side
        lo, size = halves[h]
        at = slice(lo, lo + size)
        wide = rows[slot, side, at].astype(f32)
        squares[at] += jnp.sum(wide * wide, axis=-1, keepdims=True)
        scaled = (wide * gain_ref[block]).astype(bf16)
        acc_g[at] += jnp.dot(scaled, wg[block], preferred_element_type=f32)
        acc_u[at] += jnp.dot(scaled, wu[block], preferred_element_type=f32)

    def first_half(d, carry):
        e = lax.rem(z + d, pairs)
        slot = 2 * e + y
        within(0, slot, t).wait_recv()
        along(1, e).start()
        across(0, slot).start()
        within(0, slot, t).start()
        work(0, slot, t)
        return carry

    lax.fori_loop(1, pairs, first_half, 0)
    work(0, me, t)
    work(1, me, t)

    def second_half(d, carry):
        slot = 2 * lax.rem(z + d, pairs) + y
        within(1, slot, t).wait_recv()
        across(1, slot).start()
        within(1, slot, t).start()
        work(1, slot, t)
        return carry

    lax.fori_loop(1, pairs, second_half, 0)

    def sideways(h):
        def body(d, carry):
            near = 2 * lax.rem(z + d, pairs) + y
            far = 2 * lax.rem(z + d, pairs) + 1 - y
            within(h, far, t).wait_recv()
            within(h, far, t).start()
            work(h, far, t)
            within(h, near, 1 - t).wait_recv()
            work(h, near, 1 - t)
            return carry

        lax.fori_loop(0, pairs, body, 0)

    sideways(0)
    sideways(1)

    def swapped(d, carry):
        slot = 2 * lax.rem(z + d, pairs) + 1 - y
        for h in range(2):
            within(h, slot, 1 - t).wait_recv()
            work(h, slot, 1 - t)
        return carry

    lax.fori_loop(0, pairs, swapped, 0)
    depth = 2 * pairs * 2 * width
    scale = lax.rsqrt(squares[...] / depth + norm_eps)
    gate = acc_g[...] * scale
    activated = (jax.nn.silu(gate) * (acc_u[...] * scale)).astype(bf16)
    loads[2].wait()
    first = t == 0

    def swap1(a):
        return send(send1.at[a], got1.at[a], sems1.at[0, a], sems1.at[1, a], me, 1 - t)

    for a in range(2 * pairs):
        part = jnp.dot(
            activated, wd[:, a * 2 * width : (a + 1) * 2 * width], preferred_element_type=f32
        )
        left, right = part[:, :width], part[:, width:]
        send1[a] = jnp.where(first, right, left).astype(bf16)
        swap1(a).start()
        term1[a] = jnp.where(first, left, right)

    def swap2(e):
        return send(send2.at[e], got2.at[e], sems2.at[0, e], sems2.at[1, e], beside, t)

    def reduce2(d):
        e = lax.rem(z + d, pairs)
        a = 2 * e + 1 - y
        swap1(a).wait_recv()
        send2[e] = (term1[a] + got1[a].astype(f32)).astype(bf16)
        swap2(e).start()

    reduce2(1)
    reduce2(2)

    def give3(e):
        return send(send3.at[e], got3.at[z], sems3.at[0, e], sems3.at[1, z], 2 * e + y, t)

    def take3(e):
        return send(send3.at[e], got3.at[e], sems3.at[0, e], sems3.at[1, e], 2 * e + y, t)

    def reduce3(d, carry):
        e = lax.rem(z + d, pairs)
        a = 2 * e + y
        swap1(a).wait_recv()
        swap2(e).wait_recv()

        @pl.when(d + 2 <= pairs)
        def _():
            reduce2(d + 2)

        total = (term1[a] + got1[a].astype(f32) + got2[e].astype(f32)).astype(bf16)
        send3[e] = total

        @pl.when(d < pairs)
        def _():
            give3(e).start()

        return carry

    lax.fori_loop(1, pairs + 1, reduce3, 0)
    got3[z] = send3[z]
    mixed = hidden_ref[...].astype(f32)
    for d in range(pairs):
        e = lax.rem(z + d, pairs)
        if d > 0:
            take3(e).wait_recv()
        seats = lax.broadcasted_iota(jnp.int32, (mixed.shape[0], CAP), 1) + e * CAP
        place = jnp.where(seats == target_col_ref[...], 1.0, 0.0).astype(bf16)
        mixed += jnp.dot(place, got3[e], preferred_element_type=f32)
    out_ref[...] = mixed.astype(bf16)
    for d in range(1, pairs):
        e = lax.rem(z + d, pairs)
        give3(e).wait_send()
        for h in range(2):
            along(h, e).wait_send()
    for e in range(pairs):
        swap2(e).wait_send()
        for h in range(2):
            across(h, 2 * e + y).wait_send()
    for a in range(2 * pairs):
        swap1(a).wait_send()
        for h in range(2):
            within(h, a, t).wait_send()


def run_experts(hidden, target, gain, gate, up, down, pairs):
    dma = pltpu.SemaphoreType.DMA
    tokens, width = hidden.shape
    vmem = pl.BlockSpec(memory_space=pltpu.VMEM)
    hbm = pl.BlockSpec(memory_space=pl.ANY)
    count = 2 * pairs
    units = gate.shape[1]
    blocks = (2 * count, width, units)

    def tile(*lead):
        return pltpu.VMEM(lead + (CAP, width), bf16)

    return pl.pallas_call(
        functools.partial(experts_kernel, pairs),
        out_shape=jax.ShapeDtypeStruct((tokens, width), bf16),
        in_specs=[vmem, vmem, vmem, vmem, hbm, hbm, hbm],
        out_specs=vmem,
        scratch_shapes=[
            tile(pairs),
            tile(count, 2),
            pltpu.VMEM(blocks, bf16),
            pltpu.VMEM(blocks, bf16),
            pltpu.VMEM(down.shape, bf16),
            pltpu.VMEM((CAP, units), f32),
            pltpu.VMEM((CAP, units), f32),
            pltpu.VMEM((CAP, 1), f32),
            pltpu.VMEM((count, CAP, width), f32),
            tile(count),
            tile(count),
            tile(pairs),
            tile(pairs),
            tile(pairs),
            tile(pairs),
            dma((3,)),
            dma((2, pairs)),
            dma((2, count, 2)),
            dma((2, pairs)),
            dma((2, count)),
            dma((2, count)),
            dma((2, pairs)),
            dma((2, pairs)),
        ],
        compiler_params=pltpu.CompilerParams(
            collective_id=2, has_side_effects=True, vmem_limit_bytes=56 * 2**20
        ),
    )(
        hidden, target[None, :], target[:, None], gain.reshape(2 * count, 1, width),
        gate.reshape(blocks), up.reshape(blocks), down,
    )


def on_device(
    kv_cache,
    queries,
    stream,
    page_table,
    lengths,
    send_pages,
    routes,
    value_up,
    output_weight,
    norm_gain,
    gate_weight,
    up_weight,
    down_weight,
):
    afd_count = lax.axis_size("afd")
    pairs = afd_count // 2
    t = lax.axis_index("tensor")
    pages_dev, page_len, channels = kv_cache.shape
    requests, max_pages = page_table.shape
    migrate_count = send_pages.shape[1]
    moved_total = afd_count * migrate_count
    local_count = pages_dev - moved_total
    latent = value_up.shape[1]
    each = migrate_count // 2

    give = lax.dynamic_slice_in_dim(send_pages, t * each, each, 1).reshape(-1)

    slots = jnp.arange(pages_dev, dtype=jnp.int32)
    place = jnp.arange(max_pages, dtype=jnp.int32)
    used = place[None, :] * page_len < lengths[:, None]
    match = (page_table[:, :, None] == slots) & used[:, :, None]
    owns = jnp.any(match, axis=1)
    owner = jnp.sum(
        jnp.where(owns, jnp.arange(requests, dtype=jnp.int32)[:, None], 0), axis=0
    )
    left = lengths[:, None] - place[None, :] * page_len
    limit = jnp.sum(jnp.where(match, left[:, :, None], 0), axis=(0, 1))
    part, highest, total = attend(
        kv_cache, queries, owner, limit, give, afd_count, each, local_count, latent
    )
    highest = highest[:, 0].T
    total = total[:, 0].T
    own = owns[None, :, :]
    peak = jnp.max(jnp.where(own, highest[:, None, :], -jnp.inf), axis=-1, keepdims=True)
    factor = jnp.where(own, jnp.exp(jnp.where(own, highest[:, None, :] - peak, 0.0)), 0.0)
    mass = jnp.sum(factor * total[:, None, :], axis=-1, keepdims=True)
    share = (factor / mass).astype(bf16)
    context = jnp.einsum("hrs,shl->hrl", share, part, preferred_element_type=f32).astype(bf16)
    heads_out = jnp.einsum("hrl,hlv->rhv", context, value_up, preferred_element_type=f32)
    heads_out = heads_out.astype(bf16).reshape(requests, -1)

    width = stream.shape[1] // 2
    stream_half = lax.dynamic_slice_in_dim(stream, t * width, width, 1)
    hidden = project(heads_out, output_weight, stream_half, pairs)

    route = routes[:, 0]
    onehot = (route[:, None] == jnp.arange(pairs, dtype=jnp.int32)[None, :]).astype(jnp.int32)
    rank = jnp.sum((jnp.cumsum(onehot, axis=0) - onehot) * onehot, axis=1)
    target = route * CAP + rank
    return run_experts(hidden, target, norm_gain, gate_weight, up_weight, down_weight, pairs)


def solution(mesh):
    in_specs = (
        P(("group", "afd"), None, None),
        P(("group", "afd"), "tensor", None),
        P("group", "afd"),
        P(("group", "afd"), None),
        P(("group", "afd")),
        P(("group", "afd"), None),
        P("group", None),
        P("tensor", None, None),
        P("tensor", "afd"),
        P(),
        P(None, ("afd", "tensor")),
        P(None, ("afd", "tensor")),
        P(("afd", "tensor"), None),
    )
    out_specs = P("group", ("afd", "tensor"))
    return jax.shard_map(
        on_device, mesh=mesh, in_specs=in_specs, out_specs=out_specs, check_vma=False
    )
```

```python
import functools

import jax
import jax.numpy as jnp
from jax import lax
from jax.experimental import pallas as pl
from jax.experimental.pallas import tpu as pltpu
from jax.sharding import PartitionSpec as P

CAP = 240
MESH = pl.DeviceIdType.MESH
f32 = jnp.float32
bf16 = jnp.bfloat16

score_scale = 0.07216878364870322
norm_eps = 1e-06


def send(src, dst, send_sem, recv_sem, afd, tensor):
    return pltpu.make_async_remote_copy(
        src_ref=src,
        dst_ref=dst,
        send_sem=send_sem,
        recv_sem=recv_sem,
        device_id=(lax.axis_index("group"), afd, tensor),
        device_id_type=MESH,
    )


def greet(targets):
    barrier = pltpu.get_barrier_semaphore()
    for afd, tensor in targets:
        pl.semaphore_signal(
            barrier,
            inc=1,
            device_id=(lax.axis_index("group"), afd, tensor),
            device_id_type=MESH,
        )
    pl.semaphore_wait(barrier, len(targets))


def attend_kernel(
    count, each, local, owner_ref, limit_ref, give_ref, kv_hbm, q_hbm, part_ref, top_ref, mass_ref,
    kv_ref, q_ref, load_sem, out, got, sent_sem, got_sem, pass_sem, passed_sem,
):
    me = lax.axis_index("afd")
    t = lax.axis_index("tensor")
    load_kv = pltpu.make_async_copy(kv_hbm, kv_ref, load_sem.at[0])
    load_q = pltpu.make_async_copy(q_hbm, q_ref, load_sem.at[1])
    load_kv.start()
    load_q.start()
    greet([(lax.rem(me + d, count), t) for d in range(1, count)] + [(me, 1 - t)])
    load_kv.wait()
    latent = part_ref.shape[2]

    def page_to(to):
        return send(out.at[to], got.at[me, t], sent_sem.at[to], got_sem.at[me], to, t)

    def page_from(src):
        return send(out.at[src], got.at[src, t], sent_sem.at[src], got_sem.at[src], src, t)

    def swap(src, side):
        return send(got.at[src, side], got.at[src, side], pass_sem.at[src], passed_sem.at[src], me, 1 - t)

    for d in range(1, count):
        to = lax.rem(me + d, count)
        for j in range(each):
            out[to, j] = kv_ref[give_ref[to * each + j]]
        page_to(to).start()
    for j in range(each):
        got[me, t, j] = kv_ref[give_ref[me * each + j]]
    swap(me, t).start()

    def work(items):
        scores = []
        for slot, page in items:
            product = lax.dot_general(
                page, q_ref[owner_ref[slot]], (((1,), (1,)), ((), ())), preferred_element_type=f32
            ) * score_scale
            position = lax.broadcasted_iota(jnp.int32, product.shape, 0)
            scores.append(jnp.where(position < limit_ref[slot], product, -jnp.inf))
        tops = [jnp.max(x, axis=0, keepdims=True) for x in scores]
        exponents = [jnp.exp(x - top) for x, top in zip(scores, tops)]
        masses = [jnp.sum(x, axis=0, keepdims=True) for x in exponents]
        parts = [
            lax.dot_general(
                x.astype(bf16), page[:, :latent], (((0,), (0,)), ((), ())),
                preferred_element_type=f32,
            ).astype(bf16)
            for x, (slot, page) in zip(exponents, items)
        ]
        for (slot, page), top, mass, part in zip(items, tops, masses, parts):
            top_ref[slot] = top
            mass_ref[slot] = mass
            part_ref[slot] = part

    def forward(d):
        src = lax.rem(me + d, count)
        page_from(src).wait_recv()
        swap(src, t).start()

    pace = local // count

    def resident(i, carry):
        work([(i * pace + j, kv_ref[i * pace + j]) for j in range(pace)])
        return carry

    def resident_and_forward(i, carry):
        resident(i, carry)
        forward(i)
        return carry

    load_q.wait()
    resident(0, 0)
    lax.fori_loop(1, count, resident_and_forward, 0)
    for slot in range(pace * count, local):
        work([(slot, kv_ref[slot])])

    def arrived(i, carry):
        items = []
        for d in (2 * i, 2 * i + 1):
            src = lax.rem(me + d, count)
            swap(src, 1 - t).wait_recv()
            for side in range(2):
                for j in range(each):
                    items.append((local + (src * 2 + side) * each + j, got[src, side, j]))
        work(items)
        return carry

    lax.fori_loop(0, count // 2, arrived, 0)
    for d in range(count):
        to = lax.rem(me + d, count)
        swap(to, t).wait_send()
        if d > 0:
            page_to(to).wait_send()


def attend(kv_cache, queries, owner, limit, give, count, each, local, latent):
    dma = pltpu.SemaphoreType.DMA
    slots, page_len, channels = kv_cache.shape
    heads = queries.shape[1]
    vmem = pl.BlockSpec(memory_space=pltpu.VMEM)
    smem = pl.BlockSpec(memory_space=pltpu.SMEM)
    hbm = pl.BlockSpec(memory_space=pl.ANY)
    return pl.pallas_call(
        functools.partial(attend_kernel, count, each, local),
        out_shape=(
            jax.ShapeDtypeStruct((slots, heads, latent), bf16),
            jax.ShapeDtypeStruct((slots, 1, heads), f32),
            jax.ShapeDtypeStruct((slots, 1, heads), f32),
        ),
        in_specs=[smem, smem, smem, hbm, hbm],
        out_specs=(vmem, vmem, vmem),
        scratch_shapes=[
            pltpu.VMEM(kv_cache.shape, bf16),
            pltpu.VMEM(queries.shape, bf16),
            dma((2,)),
            pltpu.VMEM((count, each, page_len, channels), bf16),
            pltpu.VMEM((count, 2, each, page_len, channels), bf16),
            dma((count,)), dma((count,)), dma((count,)), dma((count,)),
        ],
        compiler_params=pltpu.CompilerParams(
            collective_id=0, has_side_effects=True, vmem_limit_bytes=40 * 2**20
        ),
    )(owner, limit, give, kv_cache, queries)


def project_kernel(
    pairs, heads_ref, w_hbm, stream_ref, hidden_ref,
    held, w, acc, half_out, half_in, w_sem, got_sem, up_sem, down_sem, side_sem, cross_sem, half_sems,
):
    me = lax.axis_index("afd")
    t = lax.axis_index("tensor")
    z, y = me // 2, lax.rem(me, 2)
    load = pltpu.make_async_copy(w_hbm, w, w_sem)
    load.start()
    greet(
        [(2 * lax.rem(z + d, pairs) + y, t) for d in range(1, pairs)]
        + [(2 * z + 1 - y, t), (me, 1 - t)]
    )
    chunks, count, rows, step = held.shape

    def side(c, slot):
        here = held.at[c, slot]
        return send(here, here, side_sem.at[c, slot // 2], got_sem.at[c, slot], 2 * z + 1 - y, t)

    def up(c, slot):
        here = held.at[c, slot]
        return send(here, here, up_sem.at[c, slot // 2], got_sem.at[c, slot], me + 2, t)

    def down(c, slot):
        here = held.at[c, slot]
        return send(here, here, down_sem.at[c, slot // 2], got_sem.at[c, slot], me - 2, t)

    def begin(c):
        held[c, me] = heads_ref[:, c * step : (c + 1) * step]

        @pl.when(z + 1 < pairs)
        def _():
            up(c, me).start()

        @pl.when(z > 0)
        def _():
            down(c, me).start()

        side(c, me).start()

    mate = z + 1 - 2 * lax.rem(z, 2)

    def cross(c):
        here = held.at[c, 2 * z + 1 - y]
        return send(here, here, cross_sem.at[c], got_sem.at[c, 2 * z + 1 - y], 2 * mate + y, t)

    def crosses(c):
        return c % 2 == 1

    def beside(c, slot):
        if crosses(c):

            @pl.when(slot // 2 != mate)
            def _():
                side(c, slot).start()

        else:
            side(c, slot).start()

    def relay(c, s):
        if s == 1 and crosses(c):
            side(c, 2 * z + 1 - y).wait_recv()
            cross(c).start()

        @pl.when(z - s >= 0)
        def _():
            slot = me - 2 * s
            up(c, slot).wait_recv()

            @pl.when(z + 1 < pairs)
            def _():
                up(c, slot).start()

            beside(c, slot)

        @pl.when(z + s < pairs)
        def _():
            slot = me + 2 * s
            down(c, slot).wait_recv()

            @pl.when(z > 0)
            def _():
                down(c, slot).start()

            beside(c, slot)

    def finish(c):
        for a in range(pairs):
            if crosses(c):

                @pl.when(a != z)
                def _():
                    side(c, 2 * a + 1 - y).wait_recv()

            else:
                side(c, 2 * a + 1 - y).wait_recv()
        block = held[c].reshape(count * rows, step)
        acc[...] += jnp.dot(block, w[c * step : (c + 1) * step, :], preferred_element_type=f32)

    acc[...] = jnp.zeros_like(acc)
    begin(0)
    for turn in range(chunks + pairs):
        if turn + 1 < chunks:
            begin(turn + 1)
        for s in range(pairs - 1, 0, -1):
            if 0 <= turn - s < chunks:
                relay(turn - s, s)
        if turn == pairs:
            load.wait()
        if turn >= pairs:
            finish(turn - pairs)
    for c in range(chunks):
        if crosses(c):
            cross(c).wait_send()
        for a in range(pairs):
            slot = 2 * a + y
            if crosses(c):

                @pl.when(a != mate)
                def _():
                    side(c, slot).wait_send()

            else:
                side(c, slot).wait_send()

            @pl.when((a <= z) & (z + 1 < pairs))
            def _():
                up(c, slot).wait_send()

            @pl.when((a >= z) & (z > 0))
            def _():
                down(c, slot).wait_send()

    width = half_out.shape[1]
    total = acc[...]
    left, right = total[:, :width], total[:, width:]
    first = t == 0
    half_out[...] = jnp.where(first, right, left)
    swap = send(half_out, half_in, half_sems.at[0], half_sems.at[1], me, 1 - t)
    swap.start()
    mine = jnp.where(first, left, right) + stream_ref[...].astype(f32)
    swap.wait()
    hidden_ref[...] = (mine + half_in[...]).astype(bf16)


def project(heads, weight, stream_half, pairs):
    dma = pltpu.SemaphoreType.DMA
    rows, depth = heads.shape
    tokens, width = stream_half.shape
    chunks = 4
    vmem = pl.BlockSpec(memory_space=pltpu.VMEM)
    return pl.pallas_call(
        functools.partial(project_kernel, pairs),
        out_shape=jax.ShapeDtypeStruct((tokens, width), bf16),
        in_specs=[vmem, pl.BlockSpec(memory_space=pl.ANY), vmem],
        out_specs=vmem,
        scratch_shapes=[
            pltpu.VMEM((chunks, 2 * pairs, rows, depth // chunks), bf16),
            pltpu.VMEM(weight.shape, bf16),
            pltpu.VMEM((tokens, 2 * width), f32),
            pltpu.VMEM((tokens, width), f32),
            pltpu.VMEM((tokens, width), f32),
            dma,
            dma((chunks, 2 * pairs)),
            dma((chunks, pairs)),
            dma((chunks, pairs)),
            dma((chunks, pairs)),
            dma((chunks,)),
            dma((2,)),
        ],
        compiler_params=pltpu.CompilerParams(
            collective_id=1, has_side_effects=True, vmem_limit_bytes=48 * 2**20
        ),
    )(heads, weight, stream_half)


def experts_kernel(
    pairs, hidden_ref, target_row_ref, target_col_ref, gain_ref, gate_hbm, up_hbm, down_hbm, out_ref,
    buf, rows, wg, wu, wd, acc_g, acc_u, squares, term1, send1, got1, send2, got2, send3, got3,
    w_sems, z_sem, row_sem, y_sem, t_sem, sems1, sems2, sems3,
):
    me = lax.axis_index("afd")
    t = lax.axis_index("tensor")
    z, y = me // 2, lax.rem(me, 2)
    beside = 2 * z + 1 - y
    width = hidden_ref.shape[1]
    loads = [
        pltpu.make_async_copy(a, b, w_sems.at[i])
        for i, (a, b) in enumerate(((gate_hbm, wg), (up_hbm, wu), (down_hbm, wd)))
    ]
    for load in loads:
        load.start()
    greet(
        [(2 * lax.rem(z + d, pairs) + y, t) for d in range(1, pairs)]
        + [(beside, t), (me, 1 - t)]
    )

    halves = ((0, 128), (128, CAP - 128))

    def along(h, e):
        at = pl.ds(*halves[h])
        return send(buf.at[e, at], rows.at[me, t, at], z_sem.at[h, e], row_sem.at[h, me, t], 2 * e + y, t)

    def across(h, slot):
        here = rows.at[slot, t, pl.ds(*halves[h])]
        return send(here, here, y_sem.at[h, slot // 2], row_sem.at[h, slot, t], beside, t)

    def within(h, slot, side):
        here = rows.at[slot, side, pl.ds(*halves[h])]
        return send(here, here, t_sem.at[h, slot], row_sem.at[h, slot, side], me, 1 - t)

    def build(d, carry):
        e = lax.rem(z + d, pairs)
        seats = lax.broadcasted_iota(jnp.int32, (CAP, target_row_ref.shape[1]), 0) + e * CAP
        pick = jnp.where(seats == target_row_ref[...], 1.0, 0.0).astype(bf16)
        buf[e] = jnp.dot(pick, hidden_ref[...], preferred_element_type=f32).astype(bf16)

        @pl.when(d < pairs)
        def _():
            along(0, e).start()

        return carry

    lax.fori_loop(1, pairs + 1, build, 0)
    rows[me, t] = buf[z]
    for h in range(2):
        across(h, me).start()
        within(h, me, t).start()
    acc_g[...] = jnp.zeros_like(acc_g)
    acc_u[...] = jnp.zeros_like(acc_u)
    squares[...] = jnp.zeros_like(squares)
    loads[0].wait()
    loads[1].wait()

    def work(h, slot, side):
        block = slot * 2 + side
        lo, size = halves[h]
        at = slice(lo, lo + size)
        wide = rows[slot, side, at].astype(f32)
        squares[at] += jnp.sum(wide * wide, axis=-1, keepdims=True)
        scaled = (wide * gain_ref[block]).astype(bf16)
        acc_g[at] += jnp.dot(scaled, wg[block], preferred_element_type=f32)
        acc_u[at] += jnp.dot(scaled, wu[block], preferred_element_type=f32)

    def first_half(d, carry):
        e = lax.rem(z + d, pairs)
        slot = 2 * e + y
        within(0, slot, t).wait_recv()
        along(1, e).start()
        across(0, slot).start()
        within(0, slot, t).start()
        work(0, slot, t)
        return carry

    lax.fori_loop(1, pairs, first_half, 0)
    work(0, me, t)
    work(1, me, t)

    def second_half(d, carry):
        slot = 2 * lax.rem(z + d, pairs) + y
        within(1, slot, t).wait_recv()
        across(1, slot).start()
        within(1, slot, t).start()
        work(1, slot, t)
        return carry

    lax.fori_loop(1, pairs, second_half, 0)

    def sideways(h):
        def body(d, carry):
            near = 2 * lax.rem(z + d, pairs) + y
            far = 2 * lax.rem(z + d, pairs) + 1 - y
            within(h, far, t).wait_recv()
            within(h, far, t).start()
            work(h, far, t)
            within(h, near, 1 - t).wait_recv()
            work(h, near, 1 - t)
            return carry

        lax.fori_loop(0, pairs, body, 0)

    sideways(0)
    sideways(1)

    def swapped(d, carry):
        slot = 2 * lax.rem(z + d, pairs) + 1 - y
        for h in range(2):
            within(h, slot, 1 - t).wait_recv()
            work(h, slot, 1 - t)
        return carry

    lax.fori_loop(0, pairs, swapped, 0)
    depth = 2 * pairs * 2 * width
    scale = lax.rsqrt(squares[...] / depth + norm_eps)
    gate = acc_g[...] * scale
    activated = (jax.nn.silu(gate) * (acc_u[...] * scale)).astype(bf16)
    loads[2].wait()
    first = t == 0

    def swap1(a):
        return send(send1.at[a], got1.at[a], sems1.at[0, a], sems1.at[1, a], me, 1 - t)

    for a in range(2 * pairs):
        part = jnp.dot(
            activated, wd[:, a * 2 * width : (a + 1) * 2 * width], preferred_element_type=f32
        )
        left, right = part[:, :width], part[:, width:]
        send1[a] = jnp.where(first, right, left).astype(bf16)
        swap1(a).start()
        term1[a] = jnp.where(first, left, right)

    def swap2(e):
        return send(send2.at[e], got2.at[e], sems2.at[0, e], sems2.at[1, e], beside, t)

    def reduce2(d):
        e = lax.rem(z + d, pairs)
        a = 2 * e + 1 - y
        swap1(a).wait_recv()
        send2[e] = (term1[a] + got1[a].astype(f32)).astype(bf16)
        swap2(e).start()

    reduce2(1)
    reduce2(2)

    def give3(e):
        return send(send3.at[e], got3.at[z], sems3.at[0, e], sems3.at[1, z], 2 * e + y, t)

    def take3(e):
        return send(send3.at[e], got3.at[e], sems3.at[0, e], sems3.at[1, e], 2 * e + y, t)

    def reduce3(d, carry):
        e = lax.rem(z + d, pairs)
        a = 2 * e + y
        swap1(a).wait_recv()
        swap2(e).wait_recv()

        @pl.when(d + 2 <= pairs)
        def _():
            reduce2(d + 2)

        total = (term1[a] + got1[a].astype(f32) + got2[e].astype(f32)).astype(bf16)
        send3[e] = total

        @pl.when(d < pairs)
        def _():
            give3(e).start()

        return carry

    lax.fori_loop(1, pairs + 1, reduce3, 0)
    got3[z] = send3[z]
    mixed = hidden_ref[...].astype(f32)
    for d in range(pairs):
        e = lax.rem(z + d, pairs)
        if d > 0:
            take3(e).wait_recv()
        seats = lax.broadcasted_iota(jnp.int32, (mixed.shape[0], CAP), 1) + e * CAP
        place = jnp.where(seats == target_col_ref[...], 1.0, 0.0).astype(bf16)
        mixed += jnp.dot(place, got3[e], preferred_element_type=f32)
    out_ref[...] = mixed.astype(bf16)
    for d in range(1, pairs):
        e = lax.rem(z + d, pairs)
        give3(e).wait_send()
        for h in range(2):
            along(h, e).wait_send()
    for e in range(pairs):
        swap2(e).wait_send()
        for h in range(2):
            across(h, 2 * e + y).wait_send()
    for a in range(2 * pairs):
        swap1(a).wait_send()
        for h in range(2):
            within(h, a, t).wait_send()


def run_experts(hidden, target, gain, gate, up, down, pairs):
    dma = pltpu.SemaphoreType.DMA
    tokens, width = hidden.shape
    vmem = pl.BlockSpec(memory_space=pltpu.VMEM)
    hbm = pl.BlockSpec(memory_space=pl.ANY)
    count = 2 * pairs
    units = gate.shape[1]
    blocks = (2 * count, width, units)

    def tile(*lead):
        return pltpu.VMEM(lead + (CAP, width), bf16)

    return pl.pallas_call(
        functools.partial(experts_kernel, pairs),
        out_shape=jax.ShapeDtypeStruct((tokens, width), bf16),
        in_specs=[vmem, vmem, vmem, vmem, hbm, hbm, hbm],
        out_specs=vmem,
        scratch_shapes=[
            tile(pairs),
            tile(count, 2),
            pltpu.VMEM(blocks, bf16),
            pltpu.VMEM(blocks, bf16),
            pltpu.VMEM(down.shape, bf16),
            pltpu.VMEM((CAP, units), f32),
            pltpu.VMEM((CAP, units), f32),
            pltpu.VMEM((CAP, 1), f32),
            pltpu.VMEM((count, CAP, width), f32),
            tile(count),
            tile(count),
            tile(pairs),
            tile(pairs),
            tile(pairs),
            tile(pairs),
            dma((3,)),
            dma((2, pairs)),
            dma((2, count, 2)),
            dma((2, pairs)),
            dma((2, count)),
            dma((2, count)),
            dma((2, pairs)),
            dma((2, pairs)),
        ],
        compiler_params=pltpu.CompilerParams(
            collective_id=2, has_side_effects=True, vmem_limit_bytes=56 * 2**20
        ),
    )(
        hidden, target[None, :], target[:, None], gain.reshape(2 * count, 1, width),
        gate.reshape(blocks), up.reshape(blocks), down,
    )


def on_device(
    kv_cache,
    queries,
    stream,
    page_table,
    lengths,
    send_pages,
    routes,
    value_up,
    output_weight,
    norm_gain,
    gate_weight,
    up_weight,
    down_weight,
):
    afd_count = lax.axis_size("afd")
    pairs = afd_count // 2
    t = lax.axis_index("tensor")
    pages_dev, page_len, channels = kv_cache.shape
    requests, max_pages = page_table.shape
    migrate_count = send_pages.shape[1]
    moved_total = afd_count * migrate_count
    local_count = pages_dev - moved_total
    latent = value_up.shape[1]
    each = migrate_count // 2

    give = lax.dynamic_slice_in_dim(send_pages, t * each, each, 1).reshape(-1)

    slots = jnp.arange(pages_dev, dtype=jnp.int32)
    place = jnp.arange(max_pages, dtype=jnp.int32)
    used = place[None, :] * page_len < lengths[:, None]
    match = (page_table[:, :, None] == slots) & used[:, :, None]
    owns = jnp.any(match, axis=1)
    owner = jnp.sum(
        jnp.where(owns, jnp.arange(requests, dtype=jnp.int32)[:, None], 0), axis=0
    )
    left = lengths[:, None] - place[None, :] * page_len
    limit = jnp.sum(jnp.where(match, left[:, :, None], 0), axis=(0, 1))
    part, highest, total = attend(
        kv_cache, queries, owner, limit, give, afd_count, each, local_count, latent
    )
    highest = highest[:, 0].T
    total = total[:, 0].T
    own = owns[None, :, :]
    peak = jnp.max(jnp.where(own, highest[:, None, :], -jnp.inf), axis=-1, keepdims=True)
    factor = jnp.where(own, jnp.exp(jnp.where(own, highest[:, None, :] - peak, 0.0)), 0.0)
    mass = jnp.sum(factor * total[:, None, :], axis=-1, keepdims=True)
    share = (factor / mass).astype(bf16)
    context = jnp.einsum("hrs,shl->hrl", share, part, preferred_element_type=f32).astype(bf16)
    heads_out = jnp.einsum("hrl,hlv->rhv", context, value_up, preferred_element_type=f32)
    heads_out = heads_out.astype(bf16).reshape(requests, -1)

    width = stream.shape[1] // 2
    stream_half = lax.dynamic_slice_in_dim(stream, t * width, width, 1)
    hidden = project(heads_out, output_weight, stream_half, pairs)

    route = routes[:, 0]
    onehot = (route[:, None] == jnp.arange(pairs, dtype=jnp.int32)[None, :]).astype(jnp.int32)
    rank = jnp.sum((jnp.cumsum(onehot, axis=0) - onehot) * onehot, axis=1)
    target = route * CAP + rank
    return run_experts(hidden, target, norm_gain, gate_weight, up_weight, down_weight, pairs)


def solution(mesh):
    in_specs = (
        P(("group", "afd"), None, None),
        P(("group", "afd"), "tensor", None),
        P("group", "afd"),
        P(("group", "afd"), None),
        P(("group", "afd")),
        P(("group", "afd"), None),
        P("group", None),
        P("tensor", None, None),
        P("tensor", "afd"),
        P(),
        P(None, ("afd", "tensor")),
        P(None, ("afd", "tensor")),
        P(("afd", "tensor"), None),
    )
    out_specs = P("group", ("afd", "tensor"))
    return jax.shard_map(
        on_device, mesh=mesh, in_specs=in_specs, out_specs=out_specs, check_vma=False
    )
```
